256 devices in a mesh: gy: 8 (over z_hi, core), gx: 32 (over y, z_lo, x).
Axes of the slice: x: 4, y: 4, z: 8 (z_hi: 4, z_lo: 2; z = z_hi * 2 + z_lo), core: 2. Of those that a mesh axis runs over, the one named last changes fastest.
Arguments:
- nest_adjoint: float32 [50, 192, 4096], P(None, 'gy', 'gx'), may hold values from -6 to 6
- nest_kappa: float32 [2, 50, 192, 4096], P(None, None, 'gy', 'gx'), may hold values from 0.1 to 10
- nest_nu: float32 [50, 192, 4096], P(None, 'gy', 'gx'), may hold values from 0.02 to 0.24
- land_mask: int32 [192, 4096], P('gy', 'gx'), may hold values 0 or 1
- parent_adjoint: float32 [50, 384, 4096], P(None, 'gy', 'gx'), may hold values from -6 to 6
- parent_kappa: float32 [2, 50, 384, 4096], P(None, None, 'gy', 'gx'), may hold values from 0.1 to 10
- parent_traj: float32 [2, 50, 384, 4096], P(None, None, 'gy', 'gx'), may hold values from -6 to 6
- offset_row: int32 [1], replicated, may hold values from 193 to 240
- offset_col: int32 [1], replicated, may hold values from 2049 to 2176
Outputs:
- nest_result: float32 [50, 192, 4096], P(None, 'gy', 'gx')
- parent_result: float32 [50, 384, 4096], P(None, 'gy', 'gx')
- side_weights: float32 [2, 50, 2, 64], replicated
- side_gradients: float32 [2, 50, 2, 64], replicated
The draws below stay inside these ranges and needn't reach their ends.
All inputs are finite; a program needn't handle non-finite values. No bound on the sum of `land_mask` on one device may be relied on, other than what follows from the above.
Results may differ from the reference program's by a relative error of at most 0.0001.
Values sent between devices are 32-bit elements; how exact they have to be, the bound alone decides.
No kernel may reach another device: no remote copies, remote signals or barrier semaphores. Data moves between devices by JAX's collectives and lax.ppermute only.
A program may use at most 128 MiB of HBM per device.

```python
import math
import jax
import jax.numpy as jnp
from jax import lax

K = 50
R = 3
RYP = 48
RXP = 128
NYN = 192
NXN = 4096
NYP = 384
NXP = 4096
SY = 64
SX = 1366


def place_ends(drawn, rng, least, top_value):
    longest = drawn.shape.index(max(drawn.shape))
    spots = []
    for shift in (0, 1):
        where = [jax.random.randint(jax.random.fold_in(rng, axis), (), 0, length) for axis, length in enumerate(drawn.shape)]
        where[longest] = (where[longest] + shift) % drawn.shape[longest]
        spots.append(tuple(where))
    return drawn.at[spots[0]].set(least).at[spots[1]].set(top_value)


def steps_of(own_key, shape, split, low, largest):
    def one(position, parts):
        heights = jax.random.uniform(jax.random.fold_in(jax.random.fold_in(own_key, 6), position), (parts,), jnp.float32, low / len(split), largest / len(split))
        return jnp.repeat(jnp.exp(heights), shape[position] // parts).reshape((-1,) + (1,) * (len(shape) - position - 1))

    loudness = one(*split[0])
    for cut in split[1:]:
        loudness = loudness * one(*cut)
    return loudness


def bell_draw(key, extent, deviation, limit, split=(), kind=jnp.bfloat16):
    level = steps_of(key, extent, split, -0.22, 0.18) if split else 1.0
    drawn = jax.random.normal(key, extent, jnp.float32) * deviation * level
    return jnp.minimum(jnp.maximum(drawn, -limit), limit).astype(kind)


def setup_inputs(seed: int = 0) -> dict:
    streams_of = jax.random.split(jax.random.key(seed), 10)
    nest_adjoint = bell_draw(streams_of[0], (K, NYN, NXN), 1.0, 6.0, ((1, 8), (2, 32)), jnp.float32)
    nest_kappa = jnp.clip(jnp.exp(math.log(10.0) - 4.6051702 * jax.random.uniform(streams_of[1], (2, K, NYN, NXN), jnp.float32) ** steps_of(streams_of[1], (2, K, NYN, NXN), ((2, 8), (3, 32)), -0.2, 0.2)), 0.1, 10.0)
    nest_nu = jnp.clip(0.02 + 0.22 * jax.random.uniform(streams_of[2], (K, NYN, NXN), jnp.float32) ** steps_of(streams_of[2], (K, NYN, NXN), ((1, 8), (2, 32)), -0.2, 0.2), 0.02, 0.24)
    land_mask = place_ends((jax.random.randint(streams_of[3], (NYN, NXN), 0, 5) < 4).astype(jnp.int32), jax.random.fold_in(streams_of[3], 1), 0, 1)
    parent_adjoint = bell_draw(streams_of[4], (K, NYP, NXP), 1.0, 6.0, ((1, 8), (2, 32)), jnp.float32)
    parent_kappa = jnp.clip(jnp.exp(math.log(10.0) - 4.6051702 * jax.random.uniform(streams_of[5], (2, K, NYP, NXP), jnp.float32) ** steps_of(streams_of[5], (2, K, NYP, NXP), ((2, 8), (3, 32)), -0.2, 0.2)), 0.1, 10.0)
    parent_traj = bell_draw(streams_of[6], (2, K, NYP, NXP), 1.5, 6.0, ((2, 8), (3, 32)), jnp.float32)
    offset_row = jax.random.randint(streams_of[7], (1,), NYP // 2 + 1, min(NYP // 2 + RYP + 1, NYP - SY)).astype(jnp.int32)
    offset_col = jax.random.randint(streams_of[8], (1,), NXP // 2 + 1, min(NXP // 2 + RXP + 1, NXP - SX)).astype(jnp.int32)
    return {"nest_adjoint": nest_adjoint, "nest_kappa": nest_kappa, "nest_nu": nest_nu, "land_mask": land_mask, "parent_adjoint": parent_adjoint, "parent_kappa": parent_kappa, "parent_traj": parent_traj, "offset_row": offset_row, "offset_col": offset_col}


def column_solve(kappa, rhs):
    lower_c = jnp.concatenate([jnp.zeros_like(kappa[:1]), kappa[:-1]], 0)
    diag = 1.0 + lower_c + kappa
    upper_terms = jnp.concatenate([-kappa[:-1], jnp.zeros_like(kappa[:1])], 0)
    lower_terms = -lower_c
    zeros = jnp.zeros_like(rhs[0])

    def down(carry, item):
        c_prev, d_prev = carry
        diag_k, low_k, rhs_k, up_k = item
        denom = diag_k - low_k * c_prev
        c_now = up_k / denom
        d_now = (rhs_k - low_k * d_prev) / denom
        return (c_now, d_now), (c_now, d_now)

    _, (c_all, d_all) = lax.scan(down, (zeros, zeros), (diag, lower_terms, rhs, upper_terms))

    def back(x_next, item):
        c_k, d_k = item
        x_now = d_k - c_k * x_next
        return x_now, x_now

    _, solved = lax.scan(back, zeros, (c_all, d_all), reverse=True)
    return solved


def reference(nest_adjoint, nest_kappa, nest_nu, land_mask, parent_adjoint, parent_kappa, parent_traj, offset_row, offset_col):
    anchor_row = offset_row[0]
    anchor_col = offset_col[0]
    rows = jnp.arange(NYN, dtype=jnp.int32)
    cols = jnp.arange(NXN, dtype=jnp.int32)
    row_map = rows // R
    col_map = cols // R
    span_r = jnp.arange(SY, dtype=jnp.int32)
    span_c = jnp.arange(SX, dtype=jnp.int32)
    inner = (cols > 0) & (cols < NXN - 1)
    inner_float = inner.astype(jnp.float32)
    ocean = land_mask.astype(jnp.float32)
    state = nest_adjoint
    parent = parent_adjoint
    weight_list = {}
    grad_list = {}
    for step in (1, 0):
        traj = parent_traj[step]
        p_west = jax.nn.sigmoid(traj[:, anchor_row + span_r, anchor_col - 1])
        p_east = jax.nn.sigmoid(traj[:, anchor_row + span_r, anchor_col + SX])
        w_west = p_west[:, row_map]
        w_east = p_east[:, row_map]
        w_south = jax.nn.sigmoid(traj[:, anchor_row - 1, anchor_col + span_c])[:, col_map]
        w_north = jax.nn.sigmoid(traj[:, anchor_row + SY, anchor_col + span_c])[:, col_map]
        g_west = jnp.zeros((K, SY), jnp.float32).at[:, row_map].add(w_west * state[:, :, 0])
        g_east = jnp.zeros((K, SY), jnp.float32).at[:, row_map].add(w_east * state[:, :, -1])
        g_south = jnp.zeros((K, SX), jnp.float32).at[:, col_map].add(w_south * state[:, 0, :] * inner_float)
        g_north = jnp.zeros((K, SX), jnp.float32).at[:, col_map].add(w_north * state[:, -1, :] * inner_float)
        weight_list[step] = jnp.stack([p_west, p_east], 1)
        grad_list[step] = jnp.stack([g_west, g_east], 1)
        parent = parent.at[:, anchor_row + span_r, anchor_col - 1].add(g_west)
        parent = parent.at[:, anchor_row + span_r, anchor_col + SX].add(g_east)
        parent = parent.at[:, anchor_row - 1, anchor_col + span_c].add(g_south)
        parent = parent.at[:, anchor_row + SY, anchor_col + span_c].add(g_north)
        factor = jnp.where((cols == 0)[None, None, :], 1.0 - w_west[:, :, None], jnp.float32(1.0))
        factor = jnp.where((cols == NXN - 1)[None, None, :], 1.0 - w_east[:, :, None], factor)
        factor = jnp.where(((rows == 0)[:, None] & inner[None, :])[None], 1.0 - w_south[:, None, :], factor)
        factor = jnp.where(((rows == NYN - 1)[:, None] & inner[None, :])[None], 1.0 - w_north[:, None, :], factor)
        state = state * factor
        mixed = nest_nu * ocean * state
        padded = jnp.pad(mixed, ((0, 0), (1, 1), (1, 1)))
        lap = padded[:, :-2, 1:-1] + padded[:, 2:, 1:-1] + padded[:, 1:-1, :-2] + padded[:, 1:-1, 2:] - 4.0 * mixed
        state = ocean * (state + lap)
        state = column_solve(nest_kappa[step], state)
        parent = column_solve(parent_kappa[step], parent)
    side_weights = jnp.stack([weight_list[0], weight_list[1]], 0)
    side_gradients = jnp.stack([grad_list[0], grad_list[1]], 0)
    return state, parent, side_weights, side_gradients
```

```python
import jax
import jax.numpy as jnp
from jax import lax
from jax.experimental import pallas as pl
from jax.experimental.pallas import tpu as pltpu
from jax.sharding import PartitionSpec as P

R = 3
K = 50
NR = 24
PR = 48
L = 128
GY = 8
GX = 32
SR = 64
ROW0 = 192
COL0 = 2048
SOUTH = 4
WEST = 16
SPAN = 1366
F32 = jnp.float32
VM = pl.BlockSpec(memory_space=pltpu.VMEM)
SM = pl.BlockSpec(memory_space=pltpu.SMEM)
PARAMS = pltpu.CompilerParams(vmem_limit_bytes=48 * 1024 * 1024)


def exact(left, right):
    return lax.dot_general(
        left, right, (((1,), (0,)), ((), ())), precision=lax.Precision.HIGHEST, preferred_element_type=F32
    )


def exact_t(left, right):
    return lax.dot_general(
        left, right, (((1,), (1,)), ((), ())), precision=lax.Precision.HIGHEST, preferred_element_type=F32
    )


def iota(shape, dim):
    return lax.broadcasted_iota(jnp.int32, shape, dim)


def wide(col, rows):
    return jnp.broadcast_to(col, (rows, L))


def side_lane(x, ox):
    west = ox - 1 - L * x
    east = ox + SPAN - L * x
    is_west = (west >= 0) & (west < L)
    is_east = (east >= 0) & (east < L)
    return is_west, is_east, jnp.where(is_west, west, east)


def ring_row(g, oy):
    row = jnp.where(g == SOUTH, oy - 1, oy + SR) - PR * g
    return (row >= 0) & (row < PR) & (g >= SOUTH) & (g < GY - 1), row


def pack_kernel(info, a, nu, mask, traj, v_top, v_bot, v_left, v_right, pay, buf):
    g, x, oy, ox = info[0], info[1], info[2], info[3]
    m = mask[...].astype(F32)
    lane = iota((NR, L), 1)
    acc_l = jnp.zeros((NR, L), F32)
    acc_r = jnp.zeros((NR, L), F32)
    for k in range(K):
        v = nu[k] * m * a[k]
        v_top[pl.ds(k, 1), :] = v[0:1]
        v_bot[pl.ds(k, 1), :] = v[NR - 1 : NR]
        acc_l = jnp.where(lane == k, pltpu.roll(v, k, 1) if k else v, acc_l)
        acc_r = jnp.where(lane == k, pltpu.roll(v, k + 1, 1), acc_r)
    v_left[...] = acc_l
    v_right[...] = acc_r

    pay[...] = jnp.zeros(pay.shape, F32)
    row_ok, row = ring_row(g, oy)

    @pl.when(row_ok)
    def _():
        for i, s in enumerate((1, 0)):
            for k in range(K):
                pay[pl.ds(K * i + k, 1), :] = jax.nn.sigmoid(traj[s, k, pl.ds(row, 1), :])

    is_west, is_east, spot = side_lane(x, ox)

    @pl.when((is_west | is_east) & (g >= SOUTH) & (g < GY - 1))
    def _():
        plane = iota((PR, L), 1)
        acc = jnp.zeros((PR, L), F32)
        for i, s in enumerate((1, 0)):
            for k in range(K):
                to = 64 * i + k
                acc = jnp.where(plane == to, pltpu.roll(traj[s, k], lax.rem(to - spot + L, L), 1), acc)
        used = (plane < K) | ((plane >= 64) & (plane < 64 + K))
        buf[...] = jnp.zeros(buf.shape, F32)
        start = PR * g - oy + SR
        weights = jnp.where(used, jax.nn.sigmoid(acc), 0.0)
        for r in range(PR):
            buf[pl.ds(start + r, 1), :] = weights[r : r + 1]
        pay[104:168, :] = buf[SR : 2 * SR, :]


def nest_kernel(
    info, a, nu, mask, kappa, r0, r1, r2, r3, r4, r5, r6, we, h_up, h_down, h_left, h_right,
    a_out, v_top, v_bot, v_left, v_right, grad, side,
    e_s, y_s, w_s, up_s, down_s, g_s,
):
    g, x, oy, ox = info[0], info[1], info[2], info[3]
    sig = ox - COL0
    t = lax.rem(x, 3)
    rows = 104
    own = r0[0:rows, :] + r1[0:rows, :] + r2[0:rows, :]
    nxt = r3[0:rows, :] + r4[0:rows, :] + r5[0:rows, :]
    nxt2 = r6[0:rows, :]
    wl = iota((rows, L), 1)
    back = L - sig
    shift = lax.rem(back + L, L)
    panel = jnp.where(wl < back, pltpu.roll(own, shift, 1), pltpu.roll(nxt, shift, 1))
    pi, pc = iota((L, L), 0), iota((L, L), 1)
    spread = ((3 * pi <= L * t + pc) & (L * t + pc < 3 * pi + 3)).astype(F32)
    c_all = x * L + wl
    w_s[...] = jnp.where((c_all > 0) & (c_all < GX * L - 1), exact(panel, spread), 0.0)

    er, el = iota((8, L), 0), iota((8, L), 1)
    left_at = jnp.where(t == 0, -1, jnp.where(t == 1, 42, 85)) + sig
    right_at = jnp.where(t == 0, 42, jnp.where(t == 1, 85, L)) + sig
    want = jnp.where(er == 0, left_at, jnp.where(er == 1, right_at, -1))
    ends = (
        exact_t((el == want).astype(F32), own)
        + exact_t((el + L == want).astype(F32), nxt)
        + exact_t((el + 2 * L == want).astype(F32), nxt2)
    )

    row24, lane24 = iota((NR, L), 0), iota((NR, L), 1)
    m_row = (((row24 == 0) & (g == 0)) | ((row24 == NR - 1) & (g == GY - 1))).astype(F32)
    m_lane = (((lane24 == 0) & (x == 0)) | ((lane24 == L - 1) & (x == GX - 1))).astype(F32)
    ends_l = jnp.concatenate([ends[0:1], jnp.zeros((1, 24), F32)], 1)
    ends_r = jnp.concatenate([ends[1:2], jnp.zeros((1, 24), F32)], 1)
    hl = h_left[...] * (1.0 - m_row * wide(ends_l, NR))
    hr = h_right[...] * (1.0 - m_row * wide(ends_r, NR))

    panel_we = we[...]
    qr, qj = iota((NR, SR), 0), iota((NR, SR), 1)
    base = 3 * (qj - 8 * g)
    w_we = exact(((base <= qr) & (qr < base + 3)).astype(F32), panel_we)
    flip = jnp.concatenate([panel_we, jnp.zeros((SR, L), F32)], 0).T
    edge = ((pc == 0) & (x == 0)) | ((pc == L - 1) & (x == GX - 1))
    up_s[...] = h_up[...] * (1.0 - exact(flip, (edge & (pi == 8 * g - 1)).astype(F32))[0:K])
    down_s[...] = h_down[...] * (1.0 - exact(flip, (edge & (pi == 8 * g + 8)).astype(F32))[0:K])

    m = mask[...].astype(F32)
    one = jnp.ones((NR, L), F32)
    zero = jnp.zeros((NR, L), F32)
    c_prev, e_prev, y_prev = zero, zero, zero
    top = g == 0
    is31 = (x == GX - 1).astype(jnp.int32)
    for k in range(K):
        w_row = w_s[pl.ds(k, 1), :]
        raw = a[k]
        g_s[pl.ds(k, 1), :] = w_row * jnp.where(top, raw[0:1], raw[NR - 1 : NR])
        now = raw * (one - (m_row * wide(w_row, NR) + m_lane * wide(w_we[:, k : k + 1], NR)))
        v = nu[k] * m * now
        above = jnp.where(row24 == 0, wide(up_s[pl.ds(k, 1), :], NR), pltpu.roll(v, 1, 0))
        below = jnp.where(row24 == NR - 1, wide(down_s[pl.ds(k, 1), :], NR), pltpu.roll(v, NR - 1, 0))
        left = jnp.where(lane24 == 0, wide(hl[:, k : k + 1], NR), pltpu.roll(v, 1, 1))
        right = jnp.where(lane24 == L - 1, wide(hr[:, k : k + 1], NR), pltpu.roll(v, L - 1, 1))
        b = m * (now + (above + below + left + right - 4.0 * v))
        c = kappa[1, k]
        r = 1.0 / (1.0 + c + c_prev * (1.0 - e_prev))
        e = c * r
        y = (b + c_prev * y_prev) * r
        e_s[k] = e
        y_s[k] = y
        c_prev, e_prev, y_prev = c, e, y
    sol = zero
    acc_l, acc_r = zero, zero
    for k in range(K - 1, -1, -1):
        sol = y_s[k] + e_s[k] * sol if k < K - 1 else y_s[k]
        y_s[k] = sol
        w_row = w_s[pl.ds(K + k, 1), :]
        g_s[pl.ds(K + k, 1), :] = w_row * jnp.where(top, sol[0:1], sol[NR - 1 : NR])
        now = sol * (one - (m_row * wide(w_row, NR) + m_lane * wide(w_we[:, 64 + k : 65 + k], NR)))
        a_out[k] = now
        v = nu[k] * m * now
        v_top[pl.ds(k, 1), :] = v[0:1]
        v_bot[pl.ds(k, 1), :] = v[NR - 1 : NR]
        acc_l = jnp.where(lane24 == k, pltpu.roll(v, k, 1) if k else v, acc_l)
        acc_r = jnp.where(lane24 == k, pltpu.roll(v, k + 1, 1), acc_r)
    v_left[...] = acc_l
    v_right[...] = acc_r
    for i in range(2 * K, rows):
        g_s[pl.ds(i, 1), :] = jnp.zeros((1, L), F32)
    gather = ((3 * pc <= L * t + pi) & (L * t + pi < 3 * pc + 3)).astype(F32)
    grad[...] = exact(g_s[...], gather)

    side[...] = jnp.zeros(side.shape, F32)

    @pl.when((x == 0) | (x == GX - 1))
    def _():
        acc = zero
        for k in range(K):
            acc = jnp.where(lane24 == k, pltpu.roll(a[k], lax.rem(k + is31, L), 1), acc)
            acc = jnp.where(lane24 == 64 + k, pltpu.roll(y_s[k], lax.rem(64 + k + is31, L), 1), acc)
        terms = w_we * acc
        sj, sr = iota((8, NR), 0), iota((8, NR), 1)
        side[0:8, :] = exact(((3 * sj <= sr) & (sr < 3 * sj + 3)).astype(F32), terms)
        side[8:16, :] = we[pl.ds(pl.multiple_of(8 * g, 8), 8), :]


def row_kernel(info, r0, r1, r2, r3, r4, r5, out):
    sig = info[3] - COL0
    own = r0[...] + r1[...] + r2[...]
    prev = r3[...] + r4[...] + r5[...]
    shift = lax.rem(sig, L)
    out[...] = jnp.where(iota(own.shape, 1) >= sig, pltpu.roll(own, shift, 1), pltpu.roll(prev, shift, 1))


def last_kernel(
    info, a, nu, mask, kappa, h_up, h_down, h_left, h_right, q, pkappa, g_own, g_fwd, sides,
    a_out, q_out, s_w, s_g,
    e_s, pe_s, panel_s, local_s,
):
    g, x, oy, ox = info[0], info[1], info[2], info[3]
    m = mask[...].astype(F32)
    row24, lane24 = iota((NR, L), 0), iota((NR, L), 1)
    hl, hr = h_left[...], h_right[...]
    zero = jnp.zeros((NR, L), F32)
    c_prev, e_prev, y_prev = zero, zero, zero
    for k in range(K):
        now = a[k]
        v = nu[k] * m * now
        above = jnp.where(row24 == 0, wide(h_up[pl.ds(k, 1), :], NR), pltpu.roll(v, 1, 0))
        below = jnp.where(row24 == NR - 1, wide(h_down[pl.ds(k, 1), :], NR), pltpu.roll(v, NR - 1, 0))
        left = jnp.where(lane24 == 0, wide(hl[:, k : k + 1], NR), pltpu.roll(v, 1, 1))
        right = jnp.where(lane24 == L - 1, wide(hr[:, k : k + 1], NR), pltpu.roll(v, L - 1, 1))
        b = m * (now + (above + below + left + right - 4.0 * v))
        c = kappa[0, k]
        r = 1.0 / (1.0 + c + c_prev * (1.0 - e_prev))
        e = c * r
        y = (b + c_prev * y_prev) * r
        e_s[k] = e
        a_out[k] = y
        c_prev, e_prev, y_prev = c, e, y
    sol = y_prev
    for k in range(K - 2, -1, -1):
        sol = a_out[k] + e_s[k] * sol
        a_out[k] = sol

    def panels(first):
        return jnp.concatenate([sides[i, 16 * e + first : 16 * e + first + 8, :] for e in (0, 1) for i in range(GY)], 0)

    grads = panels(0)
    flip_g = grads.T
    flip_w = panels(8).T
    for i, s in enumerate((1, 0)):
        for e in (0, 1):
            s_g[s, :, e, :] = flip_g[64 * i : 64 * i + K, SR * e : SR * e + SR]
            s_w[s, :, e, :] = flip_w[64 * i : 64 * i + K, SR * e : SR * e + SR]

    q_out[...] = q[...]
    row_ok, row = ring_row(g, oy)
    is_west, is_east, spot = side_lane(x, ox)
    side_ok = (is_west | is_east) & (g >= SOUTH) & (g < GY - 1)

    @pl.when(side_ok)
    def _():
        panel_s[...] = jnp.zeros(panel_s.shape, F32)
        panel_s[SR : 2 * SR, :] = jnp.where(is_west, grads[0:SR], grads[SR : 2 * SR])
        start = PR * g - oy + SR
        for r in range(PR):
            local_s[pl.ds(r, 1), :] = panel_s[pl.ds(start + r, 1), :]

    lane48 = iota((PR, L), 1)
    for i, s in enumerate((1, 0)):

        @pl.when(row_ok)
        def _():
            for k in range(K):
                at = pl.ds(K * i + k, 1)
                q_out[k, pl.ds(row, 1), :] = q_out[k, pl.ds(row, 1), :] + (g_own[at, :] + g_fwd[at, :])

        @pl.when(side_ok)
        def _():
            for k in range(K):
                at = 64 * i + k
                q_out[k] = q_out[k] + jnp.where(lane48 == spot, wide(local_s[:, at : at + 1], PR), 0.0)

        zero = jnp.zeros((PR, L), F32)
        c_prev, e_prev, y_prev = zero, zero, zero
        for k in range(K):
            c = pkappa[s, k]
            r = 1.0 / (1.0 + c + c_prev * (1.0 - e_prev))
            e = c * r
            y = (q_out[k] + c_prev * y_prev) * r
            pe_s[k] = e
            q_out[k] = y
            c_prev, e_prev, y_prev = c, e, y
        sol = y_prev
        for k in range(K - 2, -1, -1):
            sol = q_out[k] + pe_s[k] * sol
            q_out[k] = sol


def shape(*dims):
    return jax.ShapeDtypeStruct(dims, F32)


def at(g, x):
    return g * GX + x


def moved(value, pairs):
    return lax.ppermute(value, ("gy", "gx"), pairs)


def shifted(value, axis, count, step):
    pairs = [(i, i + step) for i in range(count) if 0 <= i + step < count]
    return lax.ppermute(value, axis, pairs)


def halos(v_top, v_bot, v_left, v_right):
    return (
        shifted(v_bot, "gy", GY, 1),
        shifted(v_top, "gy", GY, -1),
        shifted(v_right, "gx", GX, 1),
        shifted(v_left, "gx", GX, -1),
    )


def on_device(nest_adjoint, nest_kappa, nest_nu, land_mask, parent_adjoint, parent_kappa, parent_traj, offset_row, offset_col):
    g = lax.axis_index("gy")
    x = lax.axis_index("gx")
    info = jnp.stack([g.astype(jnp.int32), x.astype(jnp.int32), offset_row[0], offset_col[0]])
    v_top, v_bot, v_left, v_right, pay = pl.pallas_call(
        pack_kernel,
        out_shape=(shape(K, L), shape(K, L), shape(NR, L), shape(NR, L), shape(168, L)),
        in_specs=[SM, VM, VM, VM, VM],
        out_specs=(VM,) * 5,
        scratch_shapes=[pltpu.VMEM((256, L), F32)],
        compiler_params=PARAMS,
        name="pack",
    )(info, nest_adjoint, nest_nu, land_mask, parent_traj)

    ring = range(WEST, WEST + 12)
    north = moved(pay, [(at(6, p), at(5, p)) for p in ring])
    h_up, h_down, h_left, h_right = halos(v_top, v_bot, v_left, v_right)
    pay = pay + north
    parts = []
    for t in (0, 1, 2, -3, -2, -1, -4):
        pairs = []
        for p in ring:
            j = 3 * (p - WEST) + t
            if 0 <= j < GX:
                pairs += [(at(4, p), at(0, j)), (at(5, p), at(7, j))]
        parts.append(moved(pay, pairs))
    we = parts[0][104:168]
    for part in parts[1:6]:
        we = we + part[104:168]
    for pairs in ([(0, 7), (7, 0)], [(0, 2), (7, 5)], [(0, 1), (2, 3), (5, 4), (7, 6)]):
        we = we + moved(we, [(at(i, e), at(j, e)) for i, j in pairs for e in (0, GX - 1)])

    state, v_top, v_bot, v_left, v_right, grad, side = pl.pallas_call(
        nest_kernel,
        out_shape=(
            shape(K, NR, L), shape(K, L), shape(K, L), shape(NR, L), shape(NR, L), shape(104, L), shape(16, L)
        ),
        in_specs=[SM] + [VM] * 16,
        out_specs=(VM,) * 7,
        scratch_shapes=[
            pltpu.VMEM((K, NR, L), F32), pltpu.VMEM((K, NR, L), F32), pltpu.VMEM((104, L), F32),
            pltpu.VMEM((K, L), F32), pltpu.VMEM((K, L), F32), pltpu.VMEM((104, L), F32),
        ],
        compiler_params=PARAMS,
        name="nest",
    )(info, nest_adjoint, nest_nu, land_mask, nest_kappa, *parts, we, h_up, h_down, h_left, h_right)

    h_up, h_down, h_left, h_right = halos(v_top, v_bot, v_left, v_right)
    parts = []
    for t in (0, 1, 2, -3, -2, -1):
        pairs = []
        for p in ring:
            j = 3 * (p - WEST) + t
            if 0 <= j < GX:
                pairs += [(at(0, j), at(4, p)), (at(7, j), at(5, p))]
        parts.append(moved(grad, pairs))
    g_own = pl.pallas_call(
        row_kernel,
        out_shape=shape(104, L),
        in_specs=[SM] + [VM] * 6,
        out_specs=VM,
        compiler_params=PARAMS,
        name="row",
    )(info, *parts)
    g_fwd = moved(g_own, [(at(5, p), at(6, p)) for p in ring])
    wide_side = lax.all_to_all(jnp.broadcast_to(side[None], (GX, 16, L)), "gx", 0, 0)
    pair = jnp.concatenate([wide_side[0], wide_side[GX - 1]], 0)
    sides = lax.all_to_all(jnp.broadcast_to(pair[None], (GY, 32, L)), "gy", 0, 0)

    return pl.pallas_call(
        last_kernel,
        out_shape=(shape(K, NR, L), shape(K, PR, L), shape(2, K, 2, SR), shape(2, K, 2, SR)),
        in_specs=[SM] + [VM] * 13,
        out_specs=(VM,) * 4,
        scratch_shapes=[
            pltpu.VMEM((K, NR, L), F32), pltpu.VMEM((K, PR, L), F32), pltpu.VMEM((256, L), F32), pltpu.VMEM((PR, L), F32),
        ],
        compiler_params=PARAMS,
        name="last",
    )(
        info, state, nest_nu, land_mask, nest_kappa, h_up, h_down, h_left, h_right,
        parent_adjoint, parent_kappa, g_own, g_fwd, sides,
    )


def solution(mesh):
    in_specs = (
        P(None, "gy", "gx"),
        P(None, None, "gy", "gx"),
        P(None, "gy", "gx"),
        P("gy", "gx"),
        P(None, "gy", "gx"),
        P(None, None, "gy", "gx"),
        P(None, None, "gy", "gx"),
        P(),
        P(),
    )
    out_specs = (P(None, "gy", "gx"), P(None, "gy", "gx"), P(), P())
    return jax.shard_map(on_device, mesh=mesh, in_specs=in_specs, out_specs=out_specs, check_vma=False)
```

```python
import jax
import jax.numpy as jnp
from jax import lax
from jax.experimental import pallas as pl
from jax.experimental.pallas import tpu as pltpu
from jax.sharding import PartitionSpec as P

R = 3
K = 50
NR = 24
PR = 48
L = 128
GY = 8
GX = 32
SR = 64
ROW0 = 192
COL0 = 2048
SOUTH = 4
WEST = 16
SPAN = 1366
F32 = jnp.float32
VM = pl.BlockSpec(memory_space=pltpu.VMEM)
SM = pl.BlockSpec(memory_space=pltpu.SMEM)
HB = pl.BlockSpec(memory_space=pltpu.HBM)
ANY = pl.BlockSpec(memory_space=pl.ANY)
PARAMS = pltpu.CompilerParams(vmem_limit_bytes=24 * 1024 * 1024)
FULL = pltpu.CompilerParams(vmem_limit_bytes=60 * 1024 * 1024)


def exact(left, right):
    return lax.dot_general(
        left, right, (((1,), (0,)), ((), ())), precision=lax.Precision.HIGHEST, preferred_element_type=F32
    )


def exact_t(left, right):
    return lax.dot_general(
        left, right, (((1,), (1,)), ((), ())), precision=lax.Precision.HIGHEST, preferred_element_type=F32
    )


def iota(shape, dim):
    return lax.broadcasted_iota(jnp.int32, shape, dim)


def wide(col, rows):
    return jnp.broadcast_to(col, (rows, L))


def place(row, col):
    return lax.axis_index("gy"), lax.axis_index("gx"), row[0], col[0]


def side_lane(x, ox):
    west = ox - 1 - L * x
    east = ox + SPAN - L * x
    is_west = (west >= 0) & (west < L)
    is_east = (east >= 0) & (east < L)
    return is_west, is_east, jnp.where(is_west, west, east)


def ring_row(g, x, oy):
    row = jnp.where(g == SOUTH, oy - 1, oy + SR) - PR * g
    ok = (row >= 0) & (row < PR) & (g >= SOUTH) & (g < GY - 1) & (x >= WEST) & (x < WEST + 12)
    return ok, row


def threes(x, shape, dim):
    cell = L * lax.rem(x, 3) + iota(shape, dim)
    first = 3 * iota(shape, 1 - dim)
    return ((first <= cell) & (cell < first + 3)).astype(F32)


def row_sums(rows, x):
    col = x * L + iota(rows.shape, 1)
    return exact(jnp.where((col > 0) & (col < GX * L - 1), rows, 0.0), threes(x, (L, L), 0))


def panel_kernel(o_row, o_col, traj, pay, row_s, col_s, buf, sems):
    g, x, oy, ox = place(o_row, o_col)
    row_ok, row = ring_row(g, x, oy)
    is_west, is_east, spot = side_lane(x, ox)
    side_ok = (is_west | is_east) & (g >= SOUTH) & (g < GY - 1)
    tile = pl.multiple_of(8 * (row // 8), 8)

    def row_copy():
        return pltpu.make_async_copy(traj.at[:, :, pl.ds(tile, 8), :], row_s, sems.at[2])

    def col_copy(s):
        return pltpu.make_async_copy(traj.at[s], col_s.at[s], sems.at[s])

    @pl.when(side_ok)
    def _():
        col_copy(1).start()
        col_copy(0).start()

    @pl.when(row_ok)
    def _():
        row_copy().start()

    pay[...] = jnp.zeros(pay.shape, F32)
    @pl.when(row_ok)
    def _():
        row_copy().wait()
        for i, s in enumerate((1, 0)):
            for k in range(K):
                pay[pl.ds(K * i + k, 1), :] = jax.nn.sigmoid(row_s[s, k, pl.ds(row - tile, 1), :])

    @pl.when(side_ok)
    def _():
        plane = iota((PR, L), 1)
        acc = jnp.zeros((PR, L), F32)
        for i, s in enumerate((1, 0)):
            col_copy(s).wait()
            for k in range(K):
                to = 64 * i + k
                acc = jnp.where(plane == to, pltpu.roll(col_s[s, k], lax.rem(to - spot + L, L), 1), acc)
        used = (plane < K) | ((plane >= 64) & (plane < 64 + K))
        buf[...] = jnp.zeros(buf.shape, F32)
        start = PR * g - oy + SR
        weights = jnp.where(used, jax.nn.sigmoid(acc), 0.0)
        for r in range(PR):
            buf[pl.ds(start + r, 1), :] = weights[r : r + 1]
        pay[104:168, :] = buf[SR : 2 * SR, :]


def edge_kernel(a, nu, mask, pay, to_up, to_down, v_left, v_right):
    m = mask[...].astype(F32)
    lane = iota((NR, L), 1)
    acc_l = jnp.zeros((NR, L), F32)
    acc_r = jnp.zeros((NR, L), F32)
    for k in range(K):
        v = nu[k] * m * a[k]
        to_up[pl.ds(k, 1), :] = v[0:1]
        to_down[pl.ds(k, 1), :] = v[NR - 1 : NR]
        acc_l = jnp.where(lane == k, pltpu.roll(v, k, 1) if k else v, acc_l)
        acc_r = jnp.where(lane == k, pltpu.roll(v, k + 1, 1), acc_r)
    v_left[...] = acc_l
    v_right[...] = acc_r
    for to in (to_up, to_down):
        to[K:56, :] = jnp.zeros((56 - K, L), F32)
        to[56:224, :] = pay[...]


def mix_kernel(pay, down, up, swap, after_left, after_right, out):
    g = lax.axis_index("gy")
    own = pay[0:104, :]
    out[0:104, :] = jnp.where(g == 5, own + up[56:160, :], own)
    zero = jnp.zeros((SR, L), F32)
    above = jnp.where(g == 4, zero, down[160:224, :])
    below = jnp.where(g == 6, zero, up[160:224, :])
    out[104:168, :] = pay[104:168, :] + swap[104:168, :] + above + below


def base_kernel(q, pkappa, after, q_out, e_s):
    zero = jnp.zeros((PR, L), F32)
    src = q
    for step in (1, 0):
        c_prev, e_prev, y = zero, zero, zero
        for k in range(K):
            c = pkappa[step, k]
            r = 1.0 / (1.0 + c + c_prev * (1.0 - e_prev))
            e = c * r
            e_s[k] = e
            y = (src[k] + c_prev * y) * r
            q_out[k] = y
            c_prev, e_prev = c, e
        for k in range(K - 2, -1, -1):
            y = q_out[k] + e_s[k] * y
            q_out[k] = y
        src = q_out


def spread_kernel(side, v_left, v_right, down, up, out, one_s):
    x = lax.axis_index("gx")

    def packed(v):
        return v[0:12] + pltpu.roll(v[12:24], 64, 1)

    to_left, to_right = packed(v_left[...]), packed(v_right[...])
    one_s[0:K, :] = down[56 : 56 + K, :] + up[56 : 56 + K, :]
    one_s[K:62, :] = jnp.zeros((62 - K, L), F32)
    one_s[62:78, :] = side[...]
    one_s[78:80, :] = jnp.zeros((2, L), F32)
    every = one_s[...]
    for i in range(GX):
        out[i] = every

    @pl.when(x > 0)
    def _():
        out[jnp.maximum(x - 1, 0), K:62, :] = to_left

    @pl.when(x < GX - 1)
    def _():
        out[jnp.minimum(x + 1, GX - 1), K:62, :] = to_right


def turn_kernel(across, out):
    west, east = across[0, 62:78], across[GX - 1, 62:78]
    for i in range(GY):
        out[i, 0:16] = west
        out[i, 16:32] = east


def first_lane(t):
    return jnp.where(t == 0, 0, jnp.where(t == 1, 42, 85))


def nest_kernel(
    o_row, o_col, a, nu, mask, kappa, h_up, h_down, h_left, h_right, *rest,
):
    parts = rest[:7]
    a_out, to_up, to_down, v_left, v_right, side, e_s, y_s, w_s, up_s, down_s, g_s, we_s = rest[8:]
    g, x, oy, ox = place(o_row, o_col)
    sig = ox - COL0
    t = lax.rem(x, 3)
    rows = 104
    def third(i):
        got = jnp.where(t == 0, parts[i][0:rows, :], parts[i + 1][0:rows, :])
        return jnp.where(t == 2, parts[i + 2][0:rows, :], got)

    own, nxt, nxt2 = third(0), third(3), parts[6][0:rows, :]
    wl = iota((rows, L), 1)
    back = L - sig
    shift = lax.rem(back + L, L)
    panel = jnp.where(wl < back, pltpu.roll(own, shift, 1), pltpu.roll(nxt, shift, 1))
    pi, pc = iota((L, L), 0), iota((L, L), 1)
    spread = threes(x, (L, L), 1)
    c_all = x * L + wl
    inner = (c_all > 0) & (c_all < GX * L - 1) & ((g == 0) | (g == GY - 1))
    w_s[...] = jnp.where(inner, exact(panel, spread), 0.0)

    er, el = iota((8, L), 0), iota((8, L), 1)
    left_at = jnp.where(t == 0, -1, jnp.where(t == 1, 42, 85)) + sig
    right_at = jnp.where(t == 0, 42, jnp.where(t == 1, 85, L)) + sig
    want = jnp.where(er == 0, left_at, jnp.where(er == 1, right_at, -1))
    ends = (
        exact_t((el == want).astype(F32), own)
        + exact_t((el + L == want).astype(F32), nxt)
        + exact_t((el + 2 * L == want).astype(F32), nxt2)
    )

    row24, lane24 = iota((NR, L), 0), iota((NR, L), 1)
    m_row = (((row24 == 0) & (g == 0)) | ((row24 == NR - 1) & (g == GY - 1))).astype(F32)
    m_lane = (((lane24 == 0) & (x == 0)) | ((lane24 == L - 1) & (x == GX - 1))).astype(F32)
    ends_l = jnp.concatenate([ends[0:1], jnp.zeros((1, 24), F32)], 1)
    ends_r = jnp.concatenate([ends[1:2], jnp.zeros((1, 24), F32)], 1)
    hl = h_left[...] * (1.0 - m_row * wide(ends_l, NR))
    hr = h_right[...] * (1.0 - m_row * wide(ends_r, NR))

    panel_we = parts[0][rows:, :]
    for part in parts[1:]:
        panel_we = panel_we + part[rows:, :]
    we_s[...] = panel_we
    qr, qj = iota((NR, SR), 0), iota((NR, SR), 1)
    base = 3 * (qj - 8 * g)
    w_we = exact(((base <= qr) & (qr < base + 3)).astype(F32), panel_we)
    flip = jnp.concatenate([panel_we, jnp.zeros((SR, L), F32)], 0).T
    edge = ((pc == 0) & (x == 0)) | ((pc == L - 1) & (x == GX - 1))
    up_s[...] = h_up[0:K, :] * (1.0 - exact(flip, (edge & (pi == 8 * g - 1)).astype(F32))[0:K])
    down_s[...] = h_down[0:K, :] * (1.0 - exact(flip, (edge & (pi == 8 * g + 8)).astype(F32))[0:K])

    m = mask[...].astype(F32)
    one = jnp.ones((NR, L), F32)
    zero = jnp.zeros((NR, L), F32)
    c_prev, e_prev, y = zero, zero, zero
    top = g == 0
    is31 = (x == GX - 1).astype(jnp.int32)
    for k in range(K):
        w_row = w_s[pl.ds(k, 1), :]
        raw = a[k]
        g_s[pl.ds(k, 1), :] = jnp.where(top, raw[0:1], raw[NR - 1 : NR])
        now = raw * (one - (m_row * wide(w_row, NR) + m_lane * wide(w_we[:, k : k + 1], NR)))
        v = nu[k] * m * now
        above = jnp.where(row24 == 0, wide(up_s[pl.ds(k, 1), :], NR), pltpu.roll(v, 1, 0))
        below = jnp.where(row24 == NR - 1, wide(down_s[pl.ds(k, 1), :], NR), pltpu.roll(v, NR - 1, 0))
        left = jnp.where(lane24 == 0, wide(hl[:, k : k + 1], NR), pltpu.roll(v, 1, 1))
        right = jnp.where(lane24 == L - 1, wide(hr[:, k : k + 1], NR), pltpu.roll(v, L - 1, 1))
        b = m * (now + (above + below + left + right - 4.0 * v))
        c = kappa[1, k]
        r = 1.0 / (1.0 + c + c_prev * (1.0 - e_prev))
        e = c * r
        y = (b + c_prev * y) * r
        e_s[k] = e
        y_s[k] = y
        c_prev, e_prev = c, e
    sol = zero
    acc_l, acc_r = zero, zero
    for k in range(K - 1, -1, -1):
        sol = y_s[k] + e_s[k] * sol if k < K - 1 else y_s[k]
        y_s[k] = sol
        w_row = w_s[pl.ds(K + k, 1), :]
        g_s[pl.ds(56 + k, 1), :] = jnp.where(top, sol[0:1], sol[NR - 1 : NR])
        now = sol * (one - (m_row * wide(w_row, NR) + m_lane * wide(w_we[:, 64 + k : 65 + k], NR)))
        a_out[k] = now
        v = nu[k] * m * now
        to_up[pl.ds(k, 1), :] = v[0:1]
        to_down[pl.ds(k, 1), :] = v[NR - 1 : NR]
        acc_l = jnp.where(lane24 == k, pltpu.roll(v, k, 1) if k else v, acc_l)
        acc_r = jnp.where(lane24 == k, pltpu.roll(v, k + 1, 1), acc_r)
    v_left[...] = acc_l
    v_right[...] = acc_r
    for i in (*range(K, 56), *range(56 + K, 112)):
        g_s[pl.ds(i, 1), :] = jnp.zeros((1, L), F32)
    sums = row_sums(g_s[...], x)
    sums = pltpu.roll(sums, lax.rem(L - first_lane(t), L), 1)
    sums = sums[0:56] + pltpu.roll(sums[56:112], 64, 1)
    sums = jnp.where((g == 0) | (g == GY - 1), sums, 0.0)
    for to in (to_up, to_down):
        to[K:56, :] = jnp.zeros((56 - K, L), F32)
        to[56:112, :] = sums

    side[...] = jnp.zeros(side.shape, F32)

    @pl.when((x == 0) | (x == GX - 1))
    def _():
        acc = zero
        for k in range(K):
            acc = jnp.where(lane24 == k, pltpu.roll(a[k], lax.rem(k + is31, L), 1), acc)
            acc = jnp.where(lane24 == 64 + k, pltpu.roll(y_s[k], lax.rem(64 + k + is31, L), 1), acc)
        terms = w_we * acc
        sj, sr = iota((8, NR), 0), iota((8, NR), 1)
        side[0:8, :] = exact(((3 * sj <= sr) & (sr < 3 * sj + 3)).astype(F32), terms)
        side[8:16, :] = we_s[pl.ds(pl.multiple_of(8 * g, 8), 8), :]


def last_kernel(
    o_row, o_col, a, nu, mask, kappa, across, sides, down, up, third, pay, pkappa, q,
    a_out, q_out, s_w, s_g,
    e_s, panel_s, local_s, g_s, t_s, d_s, up_s, row_k, tile_s, col_k, q_s, pe_s, sems,
):
    g, x, oy, ox = place(o_row, o_col)
    row_ok, row = ring_row(g, x, oy)
    is_west, is_east, spot = side_lane(x, ox)
    side_ok = (is_west | is_east) & (g >= SOUTH) & (g < GY - 1)
    alone = row_ok & jnp.logical_not(side_ok)
    tile = pl.multiple_of(8 * (row // 8), 8)
    at = pl.ds(tile, 8)

    def row_copy():
        return pltpu.make_async_copy(pkappa.at[:, :, at, :], row_k, sems.at[0])

    def tile_copy():
        return pltpu.make_async_copy(q.at[:, at, :], tile_s, sems.at[1])

    def col_copy():
        return pltpu.make_async_copy(pkappa, col_k, sems.at[2])

    def whole_copy():
        return pltpu.make_async_copy(q, q_s, sems.at[3])

    @pl.when(side_ok)
    def _():
        col_copy().start()
        whole_copy().start()

    @pl.when(row_ok)
    def _():
        row_copy().start()

    @pl.when(alone)
    def _():
        tile_copy().start()

    m = mask[...].astype(F32)
    row24, lane24 = iota((NR, L), 0), iota((NR, L), 1)

    def unpacked(p):
        return jnp.concatenate([p, pltpu.roll(p, 64, 1)], 0)

    hl = jnp.where(x > 0, unpacked(across[jnp.maximum(x - 1, 0), K:62]), 0.0)
    hr = jnp.where(x < GX - 1, unpacked(across[jnp.minimum(x + 1, GX - 1), K:62]), 0.0)
    up_s[...] = third[...] + jnp.where((g == 4) | (g == 5), 0.0, down[0:K, :])
    zero = jnp.zeros((NR, L), F32)
    c_prev, e_prev, y = zero, zero, zero
    for k in range(K):
        now = a[k]
        v = nu[k] * m * now
        above = jnp.where(row24 == 0, wide(up_s[pl.ds(k, 1), :], NR), pltpu.roll(v, 1, 0))
        below = jnp.where(row24 == NR - 1, wide(up[pl.ds(k, 1), :], NR), pltpu.roll(v, NR - 1, 0))
        left = jnp.where(lane24 == 0, wide(hl[:, k : k + 1], NR), pltpu.roll(v, 1, 1))
        right = jnp.where(lane24 == L - 1, wide(hr[:, k : k + 1], NR), pltpu.roll(v, L - 1, 1))
        b = m * (now + (above + below + left + right - 4.0 * v))
        c = kappa[0, k]
        r = 1.0 / (1.0 + c + c_prev * (1.0 - e_prev))
        e = c * r
        y = (b + c_prev * y) * r
        e_s[k] = e
        a_out[k] = y
        c_prev, e_prev = c, e
    for k in range(K - 2, -1, -1):
        y = a_out[k] + e_s[k] * y
        a_out[k] = y

    def panels(first):
        return jnp.concatenate([sides[i, 16 * e + first : 16 * e + first + 8, :] for e in (0, 1) for i in range(GY)], 0)

    grads = panels(0)
    flip_g = grads.T
    flip_w = panels(8).T
    for i, s in enumerate((1, 0)):
        for e in (0, 1):
            s_g[s, :, e, :] = flip_g[64 * i : 64 * i + K, SR * e : SR * e + SR]
            s_w[s, :, e, :] = flip_w[64 * i : 64 * i + K, SR * e : SR * e + SR]

    def correct(coef, terms, zero, mid_s, fact_s):
        for step in (1, 0):
            c_prev, e_prev, y = zero, zero, zero
            for k in range(K):
                c = coef[step, k]
                r = 1.0 / (1.0 + c + c_prev * (1.0 - e_prev))
                e = c * r
                fact_s[k] = e
                term = terms(step, k)
                y = ((term if step else term + mid_s[k]) + c_prev * y) * r
                mid_s[k] = y
                c_prev, e_prev = c, e
            for k in range(K - 2, -1, -1):
                y = mid_s[k] + fact_s[k] * y
                mid_s[k] = y

    @pl.when(row_ok)
    def _():
        sig = ox - COL0
        turn = lax.rem(sig, L)
        low = iota((56, L), 1) < 64

        def come(base):
            first = jnp.zeros((56, L), F32)
            second = jnp.zeros((56, L), F32)
            for t in range(3):
                j = 3 * base + t
                got = jnp.where((j >= 0) & (j < GX), across[jnp.clip(j, 0, GX - 1), 0:56], 0.0)
                one = jnp.where(low, got, 0.0)
                two = jnp.where(low, pltpu.roll(got, 64, 1), 0.0)
                start = (0, 42, 85)[t]
                first = first + (pltpu.roll(one, start, 1) if t else one)
                second = second + (pltpu.roll(two, start, 1) if t else two)
            return first, second

        def on_parent(own, prev):
            return jnp.where(iota(own.shape, 1) >= sig, pltpu.roll(own, turn, 1), pltpu.roll(prev, turn, 1))

        own, prev = come(x - WEST), come(x - WEST - 1)
        g_s[0:56, :] = on_parent(own[0], prev[0]) * pay[0:56, :]
        g_s[K : 2 * K, :] = on_parent(own[1], prev[1])[0:K] * pay[K : 2 * K, :]
        here = iota((8, L), 0) == row - tile
        row_copy().wait()
        correct(
            row_k,
            lambda step, k: jnp.where(here, wide(g_s[pl.ds(k if step else K + k, 1), :], 8), 0.0),
            jnp.zeros((8, L), F32), t_s, pe_s.at[:, 0:8, :],
        )

    @pl.when(alone)
    def _():
        tile_copy().wait()
        t_s[...] = t_s[...] + tile_s[...]
        back = pltpu.make_async_copy(t_s, q_out.at[:, at, :], sems.at[1])
        back.start()
        back.wait()

    @pl.when(side_ok)
    def _():
        panel_s[...] = jnp.zeros(panel_s.shape, F32)
        panel_s[SR : 2 * SR, :] = jnp.where(is_west, grads[0:SR], grads[SR : 2 * SR])
        start = PR * g - oy + SR
        for r in range(PR):
            local_s[pl.ds(r, 1), :] = panel_s[pl.ds(start + r, 1), :]
        here = iota((PR, L), 1) == spot
        local = local_s[...]

        def terms(step, k):
            i = k if step else 64 + k
            return jnp.where(here, wide(local[:, i : i + 1], PR), 0.0)

        col_copy().wait()
        correct(col_k, terms, jnp.zeros((PR, L), F32), d_s, pe_s)
        whole_copy().wait()
        d_s[...] = d_s[...] + q_s[...]

        @pl.when(row_ok)
        def _():
            for k in range(K):
                d_s[k, at, :] = d_s[k, at, :] + t_s[k]

        back = pltpu.make_async_copy(d_s, q_out, sems.at[3])
        back.start()
        back.wait()


def shape(*dims):
    return jax.ShapeDtypeStruct(dims, F32)


def at(g, x):
    return g * GX + x


def moved(value, pairs):
    return lax.ppermute(value, ("gy", "gx"), pairs)


def shifted(value, axis, count, step):
    pairs = [(i, i + step) for i in range(count) if 0 <= i + step < count]
    return lax.ppermute(value, axis, pairs)


TURNS = (0, 1, 2, -3, -2, -1, -4)


def panel_routes():
    routes = []
    for t in TURNS:
        pairs = []
        for p in range(WEST, WEST + 12):
            j = 3 * (p - WEST) + t
            if 0 <= j < GX:
                pairs += [(at(4, p), at(0, j)), (at(5, p), at(7, j))]
        routes.append(pairs)
    for e, p in ((0, WEST), (GX - 1, WEST + 10), (GX - 1, WEST + 11)):
        for k in range(1, GY - 1):
            free = [
                (n, i)
                for i in (6, 5, 4)
                for n, pairs in enumerate(routes)
                if not any(a == at(i, p) or b == at(k, e) for a, b in pairs)
            ]
            n, i = free[0]
            routes[n].append((at(i, p), at(k, e)))
    return routes


def on_device(nest_adjoint, nest_kappa, nest_nu, land_mask, parent_adjoint, parent_kappa, parent_traj, offset_row, offset_col):
    here = (offset_row, offset_col)
    pay = pl.pallas_call(
        panel_kernel,
        out_shape=shape(168, L),
        in_specs=[SM, SM, HB],
        out_specs=VM,
        scratch_shapes=[
            pltpu.VMEM((2, K, 8, L), F32), pltpu.VMEM((2, K, PR, L), F32), pltpu.VMEM((256, L), F32),
            pltpu.SemaphoreType.DMA((3,)),
        ],
        compiler_params=FULL,
        name="panel",
    )(*here, parent_traj)
    to_up, to_down, v_left, v_right = pl.pallas_call(
        edge_kernel,
        out_shape=(shape(224, L), shape(224, L), shape(NR, L), shape(NR, L)),
        in_specs=[VM] * 4,
        out_specs=(VM,) * 4,
        compiler_params=PARAMS,
        name="edge",
    )(nest_adjoint, nest_nu, land_mask, pay)
    down = shifted(to_down, "gy", GY, 1)
    up = shifted(to_up, "gy", GY, -1)
    ring = range(WEST, WEST + 12)
    swap = moved(pay, [(at(i, p), at(10 - i, p)) for i in (4, 6) for p in ring])
    h_left = shifted(v_right, "gx", GX, 1)
    h_right = shifted(v_left, "gx", GX, -1)
    mixed = pl.pallas_call(
        mix_kernel,
        out_shape=shape(168, L),
        in_specs=[VM] * 4 + [ANY] * 2,
        out_specs=VM,
        compiler_params=PARAMS,
        name="mix",
    )(pay, down, up, swap, h_left, h_right)
    parts = [moved(mixed, pairs) for pairs in panel_routes()]
    nest, parent = shape(K, NR, L), shape(K, PR, L)
    base = pl.pallas_call(
        base_kernel,
        out_shape=parent,
        in_specs=[VM] * 2 + [ANY],
        out_specs=VM,
        scratch_shapes=[pltpu.VMEM((K, PR, L), F32)],
        compiler_params=PARAMS,
        cost_estimate=pl.CostEstimate(flops=10000000, bytes_accessed=12000000, transcendentals=0),
        name="base",
    )(parent_adjoint, parent_kappa, mixed)

    state, to_up, to_down, v_left, v_right, side = pl.pallas_call(
        nest_kernel,
        out_shape=(nest, shape(112, L), shape(112, L), shape(NR, L), shape(NR, L), shape(16, L)),
        in_specs=[SM] * 2 + [VM] * 15 + [ANY],
        out_specs=(VM,) * 6,
        scratch_shapes=[
            pltpu.VMEM((K, NR, L), F32), pltpu.VMEM((K, NR, L), F32), pltpu.VMEM((104, L), F32), pltpu.VMEM((K, L), F32),
            pltpu.VMEM((K, L), F32), pltpu.VMEM((112, L), F32), pltpu.VMEM((SR, L), F32),
        ],
        compiler_params=PARAMS,
        name="nest",
    )(*here, nest_adjoint, nest_nu, land_mask, nest_kappa, down, up, h_left, h_right, *parts, base)

    rows = ((0, 4), (7, 5), (1, 2), (2, 3), (5, 6), (6, 7))
    down = moved(to_down, [(at(i, j), at(k, j)) for i, k in rows for j in range(GX)])
    up = shifted(to_up, "gy", GY, -1)
    third = moved(to_down[0:K], [(at(i, j), at(i + 1, j)) for i in (0, 3, 4) for j in range(GX)])
    across = pl.pallas_call(
        spread_kernel,
        out_shape=shape(GX, 80, L),
        in_specs=[VM] * 5,
        out_specs=VM,
        scratch_shapes=[pltpu.VMEM((80, L), F32)],
        compiler_params=PARAMS,
        name="spread",
    )(side, v_left, v_right, down, up)
    across = lax.all_to_all(across, "gx", 0, 0)
    sides = pl.pallas_call(
        turn_kernel, out_shape=shape(GY, 32, L), in_specs=[VM], out_specs=VM, compiler_params=PARAMS, name="turn"
    )(across)
    sides = lax.all_to_all(sides, "gy", 0, 0)

    return pl.pallas_call(
        last_kernel,
        out_shape=(nest, parent, shape(2, K, 2, SR), shape(2, K, 2, SR)),
        in_specs=[SM] * 2 + [VM] * 10 + [HB] * 2,
        out_specs=(VM, HB, VM, VM),
        scratch_shapes=[
            pltpu.VMEM((K, NR, L), F32), pltpu.VMEM((256, L), F32), pltpu.VMEM((PR, L), F32), pltpu.VMEM((104, L), F32),
            pltpu.VMEM((K, 8, L), F32), pltpu.VMEM((K, PR, L), F32), pltpu.VMEM((K, L), F32),
            pltpu.VMEM((2, K, 8, L), F32), pltpu.VMEM((K, 8, L), F32), pltpu.VMEM((2, K, PR, L), F32),
            pltpu.VMEM((K, PR, L), F32), pltpu.VMEM((K, PR, L), F32), pltpu.SemaphoreType.DMA((4,)),
        ],
        input_output_aliases={13: 1},
        compiler_params=PARAMS,
        name="last",
    )(*here, state, nest_nu, land_mask, nest_kappa, across, sides, down, up, third, pay, parent_kappa, base)


def solution(mesh):
    in_specs = (
        P(None, "gy", "gx"),
        P(None, None, "gy", "gx"),
        P(None, "gy", "gx"),
        P("gy", "gx"),
        P(None, "gy", "gx"),
        P(None, None, "gy", "gx"),
        P(None, None, "gy", "gx"),
        P(),
        P(),
    )
    out_specs = (P(None, "gy", "gx"), P(None, "gy", "gx"), P(), P())
    return jax.shard_map(on_device, mesh=mesh, in_specs=in_specs, out_specs=out_specs, check_vma=False)
```

```python
import jax
import jax.numpy as jnp
from jax import lax
from jax.experimental import pallas as pl
from jax.experimental.pallas import tpu as pltpu
from jax.sharding import PartitionSpec as P

R = 3
K = 50
NR = 24
PR = 48
L = 128
GY = 8
GX = 32
SR = 64
ROW0 = 192
COL0 = 2048
SOUTH = 4
WEST = 16
SPAN = 1366
F32 = jnp.float32
VM = pl.BlockSpec(memory_space=pltpu.VMEM)
SM = pl.BlockSpec(memory_space=pltpu.SMEM)
HB = pl.BlockSpec(memory_space=pltpu.HBM)
ANY = pl.BlockSpec(memory_space=pl.ANY)


def grant(mib):
    return pltpu.CompilerParams(vmem_limit_bytes=mib * 1024 * 1024)


TURNS = (0, 1, 2, -3, -2, -1, -4)
SEVENTH = ((WEST, 4), (WEST + 10, 2), (WEST + 11, 0))


def side_round(i, g):
    return jnp.where(g == GY - 1, SEVENTH[i][1], lax.rem((1, 3, 5)[i] + g, 7))


def exact(left, right):
    return lax.dot_general(
        left, right, (((1,), (0,)), ((), ())), precision=lax.Precision.HIGHEST, preferred_element_type=F32
    )


def exact_t(left, right):
    return lax.dot_general(
        left, right, (((1,), (1,)), ((), ())), precision=lax.Precision.HIGHEST, preferred_element_type=F32
    )


def iota(shape, dim):
    return lax.broadcasted_iota(jnp.int32, shape, dim)


def wide(col, rows):
    return jnp.broadcast_to(col, (rows, L))


def place(row, col):
    return lax.axis_index("gy"), lax.axis_index("gx"), row[0], col[0]


def side_lane(x, ox):
    west = ox - 1 - L * x
    east = ox + SPAN - L * x
    is_west = (west >= 0) & (west < L)
    is_east = (east >= 0) & (east < L)
    return is_west, is_east, jnp.where(is_west, west, east)


def ring_row(g, x, oy):
    row = jnp.where(g == SOUTH, oy - 1, oy + SR) - PR * g
    ok = (row >= 0) & (row < PR) & (g >= SOUTH) & (g < GY - 1) & (x >= WEST) & (x < WEST + 12)
    return ok, row


def threes(x, shape, dim):
    cell = L * lax.rem(x, 3) + iota(shape, dim)
    first = 3 * iota(shape, 1 - dim)
    return ((first <= cell) & (cell < first + 3)).astype(F32)


def row_sums(rows, x):
    col = x * L + iota(rows.shape, 1)
    return exact(jnp.where((col > 0) & (col < GX * L - 1), rows, 0.0), threes(x, (L, L), 0))


def edge_kernel(o_row, o_col, a, nu, mask, traj, to_up, to_down, v_left, v_right, pay, row_s, col_s, buf, sems):
    g, x, oy, ox = place(o_row, o_col)
    row_ok, row = ring_row(g, x, oy)
    is_west, is_east, spot = side_lane(x, ox)
    side_ok = (is_west | is_east) & (g >= SOUTH) & (g < GY - 1)
    tile = pl.multiple_of(8 * (row // 8), 8)

    def row_copy():
        return pltpu.make_async_copy(traj.at[:, :, pl.ds(tile, 8), :], row_s, sems.at[2])

    def col_copy(s):
        return pltpu.make_async_copy(traj.at[s], col_s.at[s], sems.at[s])

    @pl.when(side_ok)
    def _():
        col_copy(1).start()
        col_copy(0).start()

    @pl.when(row_ok)
    def _():
        row_copy().start()

    m = mask[...].astype(F32)
    lane = iota((NR, L), 1)
    acc_l = jnp.zeros((NR, L), F32)
    acc_r = jnp.zeros((NR, L), F32)
    for k in range(K):
        v = nu[k] * m * a[k]
        to_up[pl.ds(k, 1), :] = v[0:1]
        to_down[pl.ds(k, 1), :] = v[NR - 1 : NR]
        acc_l = jnp.where(lane == k, pltpu.roll(v, k, 1) if k else v, acc_l)
        acc_r = jnp.where(lane == k, pltpu.roll(v, k + 1, 1), acc_r)
    v_left[...] = acc_l
    v_right[...] = acc_r
    pay[...] = jnp.zeros(pay.shape, F32)

    @pl.when(row_ok)
    def _():
        row_copy().wait()
        for i, s in enumerate((1, 0)):
            for k in range(K):
                pay[pl.ds(K * i + k, 1), :] = jax.nn.sigmoid(row_s[s, k, pl.ds(row - tile, 1), :])

    @pl.when(side_ok)
    def _():
        plane = iota((PR, L), 1)
        acc = jnp.zeros((PR, L), F32)
        for i, s in enumerate((1, 0)):
            col_copy(s).wait()
            for k in range(K):
                to = 64 * i + k
                acc = jnp.where(plane == to, pltpu.roll(col_s[s, k], lax.rem(to - spot + L, L), 1), acc)
        used = (plane < K) | ((plane >= 64) & (plane < 64 + K))
        buf[...] = jnp.zeros(buf.shape, F32)
        start = PR * g - oy + SR
        weights = jnp.where(used, jax.nn.sigmoid(acc), 0.0)
        for r in range(PR):
            buf[pl.ds(start + r, 1), :] = weights[r : r + 1]
        pay[104:168, :] = buf[SR : 2 * SR, :]

    for to in (to_up, to_down):
        to[K:56, :] = jnp.zeros((56 - K, L), F32)
    to_down[56:120, :] = pay[104:168, :]


def mix_kernel(o_col, pay, down, skip, after_left, after_right, *outs):
    g, x = lax.axis_index("gy"), lax.axis_index("gx")
    sig = o_col[0] - COL0
    own = pay[0:104, :] + jnp.where(g == 5, skip[0:104, :], 0.0)
    sides = pay[104:168, :] + down[56:120, :] + skip[104:168, :]
    lane = iota((K, L), 1)
    spare = jnp.zeros((64 - K, L), F32)
    for i, (t, out) in enumerate(zip(TURNS, outs)):
        begin = (0, 42, 85)[t % 3] - 1 + L * (t // 3) + sig
        turn = lax.rem(4 * L - begin, L)
        cell = begin + lane
        one = jnp.where((lane < 48) & (cell >= 0) & (cell < L), pltpu.roll(own[0:K], turn, 1), 0.0)
        cell = cell - 64
        two = jnp.where(
            (lane >= 64) & (lane < 112) & (cell >= 0) & (cell < L), pltpu.roll(own[K : 2 * K], lax.rem(turn + 64, L), 1), 0.0
        )
        part = jnp.concatenate([one + two, spare], 0)
        extra = g == 6
        for p, n in SEVENTH:
            extra = extra | ((g == 5) & (x == p) & (n == i))
        out[...] = jnp.where(extra, sides, part)


def base_kernel(o_row, o_col, q, pkappa, after, q_out, row_k, col_c, col_r, e_s, r_s):
    g, x, oy, ox = place(o_row, o_col)
    zero = jnp.zeros((PR, L), F32)
    src = q
    for step in (1, 0):
        c_prev, e_prev, y = zero, zero, zero
        for k in range(K):
            c = pkappa[step, k]
            r = 1.0 / (1.0 + c + c_prev * (1.0 - e_prev))
            e = c * r
            e_s[k] = e
            r_s[step, k] = r
            y = (src[k] + c_prev * y) * r
            q_out[k] = y
            c_prev, e_prev = c, e
        for k in range(K - 2, -1, -1):
            y = q_out[k] + e_s[k] * y
            q_out[k] = y
        src = q_out
    row_ok, row = ring_row(g, x, oy)
    is_west, is_east, spot = side_lane(x, ox)

    @pl.when(row_ok)
    def _():
        row_k[...] = pkappa[:, :, pl.ds(pl.multiple_of(8 * (row // 8), 8), 8), :]

    @pl.when(is_west | is_east)
    def _():
        lane = iota((PR, L), 1)
        for values, out in ((pkappa, col_c), (r_s, col_r)):
            acc = zero
            for i, s in enumerate((1, 0)):
                for k in range(K):
                    to = 64 * i + k
                    acc = jnp.where(lane == to, pltpu.roll(values[s, k], lax.rem(to - spot + L, L), 1), acc)
            out[...] = acc


def spread_kernel(side, v_left, v_right, down, up, after, out, one_s):
    x = lax.axis_index("gx")

    def packed(v):
        return v[0:12] + pltpu.roll(v[12:24], 64, 1)

    to_left, to_right = packed(v_left[...]), packed(v_right[...])
    one_s[0:K, :] = down[56 : 56 + K, :] + up[56 : 56 + K, :]
    one_s[K:62, :] = jnp.zeros((62 - K, L), F32)
    one_s[62:78, :] = side[...]
    one_s[78:80, :] = jnp.zeros((2, L), F32)
    every = one_s[...]
    for i in range(GX):
        out[i] = every

    @pl.when(x > 0)
    def _():
        out[jnp.maximum(x - 1, 0), K:62, :] = to_left

    @pl.when(x < GX - 1)
    def _():
        out[jnp.minimum(x + 1, GX - 1), K:62, :] = to_right


def turn_kernel(across, out):
    west, east = across[0, 62:78], across[GX - 1, 62:78]
    for i in range(GY):
        out[i, 0:16] = west
        out[i, 16:32] = east


def first_lane(t):
    return jnp.where(t == 0, 0, jnp.where(t == 1, 42, 85))


def nest_kernel(
    o_row, o_col, a, nu, mask, kappa, h_up, h_down, h_left, h_right, *rest,
):
    parts = rest[:7]
    a_out, to_up, to_down, v_left, v_right, side, e_s, y_s, w_s, up_s, down_s, g_s, we_s, w24_s = rest[8:]
    g, x, oy, ox = place(o_row, o_col)
    t = lax.rem(x, 3)
    def pick(i):
        got = jnp.where(t == 0, parts[i][...], parts[i + 1][...])
        return jnp.where(t == 2, parts[i + 2][...], got)

    window = (pick(0) + pick(3) + jnp.where(t == 2, parts[6][...], 0.0))[0:56]
    wl = iota((56, L), 1)
    low = wl < 64
    panel = jnp.concatenate([jnp.where(low, window, 0.0), jnp.where(low, pltpu.roll(window, 64, 1), 0.0)], 0)
    shift = first_lane(t) - 1
    si, sc = iota((L, L), 0) + shift, L * t + iota((L, L), 1)
    spread = ((3 * si <= sc) & (sc < 3 * si + 3)).astype(F32)
    c_all = x * L + iota((112, L), 1)
    inner = (c_all > 0) & (c_all < GX * L - 1) & ((g == 0) | (g == GY - 1))
    w_s[...] = jnp.where(inner, exact(panel, spread), 0.0)

    er, el = iota((8, L), 0), iota((8, L), 1)
    want = jnp.where(er == 0, jnp.where(t == 0, 0, 1), jnp.where(er == 1, jnp.where(t == 0, 43, 44), -1))
    ends = exact_t((el == want).astype(F32), panel[0:56])

    row24, lane24 = iota((NR, L), 0), iota((NR, L), 1)
    m_row = (((row24 == 0) & (g == 0)) | ((row24 == NR - 1) & (g == GY - 1))).astype(F32)
    m_lane = (((lane24 == 0) & (x == 0)) | ((lane24 == L - 1) & (x == GX - 1))).astype(F32)
    ends_l = jnp.concatenate([ends[0:1], jnp.zeros((1, L - 56), F32)], 1)
    ends_r = jnp.concatenate([ends[1:2], jnp.zeros((1, L - 56), F32)], 1)
    hl = h_left[...] * (1.0 - m_row * wide(ends_l, NR))
    hr = h_right[...] * (1.0 - m_row * wide(ends_r, NR))

    panel_we = jnp.zeros((SR, L), F32)
    for i, part in enumerate(parts):
        come = ((x == 0) & (side_round(0, g) == i)) | (
            (x == GX - 1) & ((side_round(1, g) == i) | (side_round(2, g) == i))
        )
        panel_we = panel_we + jnp.where(come, part[...], 0.0)
    we_s[...] = panel_we
    mine = we_s[pl.ds(pl.multiple_of(8 * g, 8), 8), :]
    for i in range(8):
        w24_s[3 * i : 3 * i + 3, :] = jnp.broadcast_to(mine[i : i + 1], (3, L))
    w_we = w24_s[...]
    flip = jnp.concatenate([panel_we, jnp.zeros((SR, L), F32)], 0).T[0:56]
    spot = jnp.where(x == 0, 0, L - 1)
    lane56 = iota((56, L), 1)
    edge = (lane56 == spot) & ((x == 0) | (x == GX - 1))
    w_up = jnp.where(edge & (g > 0), pltpu.roll(flip, lax.rem(spot - (8 * g - 1) + L, L), 1), 0.0)
    w_down = jnp.where(edge & (g < GY - 1), pltpu.roll(flip, lax.rem(spot - (8 * g + 8) + L, L), 1), 0.0)
    up_s[...] = h_up[0:K, :] * (1.0 - w_up[0:K])
    down_s[...] = h_down[0:K, :] * (1.0 - w_down[0:K])

    m = mask[...].astype(F32)
    one = jnp.ones((NR, L), F32)
    zero = jnp.zeros((NR, L), F32)
    c_prev, e_prev, y = zero, zero, zero
    top = g == 0
    is31 = (x == GX - 1).astype(jnp.int32)
    for k in range(K):
        w_row = w_s[pl.ds(k, 1), :]
        raw = a[k]
        g_s[pl.ds(k, 1), :] = jnp.where(top, raw[0:1], raw[NR - 1 : NR])
        now = raw * (one - (m_row * wide(w_row, NR) + m_lane * wide(w_we[:, k : k + 1], NR)))
        v = nu[k] * m * now
        above = jnp.where(row24 == 0, wide(up_s[pl.ds(k, 1), :], NR), pltpu.roll(v, 1, 0))
        below = jnp.where(row24 == NR - 1, wide(down_s[pl.ds(k, 1), :], NR), pltpu.roll(v, NR - 1, 0))
        left = jnp.where(lane24 == 0, wide(hl[:, k : k + 1], NR), pltpu.roll(v, 1, 1))
        right = jnp.where(lane24 == L - 1, wide(hr[:, k : k + 1], NR), pltpu.roll(v, L - 1, 1))
        b = m * (now + (above + below + left + right - 4.0 * v))
        c = kappa[1, k]
        r = 1.0 / (1.0 + c + c_prev * (1.0 - e_prev))
        e = c * r
        y = (b + c_prev * y) * r
        e_s[k] = e
        y_s[k] = y
        c_prev, e_prev = c, e
    sol = zero
    acc_l, acc_r = zero, zero
    for k in range(K - 1, -1, -1):
        sol = y_s[k] + e_s[k] * sol if k < K - 1 else y_s[k]
        y_s[k] = sol
        w_row = w_s[pl.ds(56 + k, 1), :]
        g_s[pl.ds(56 + k, 1), :] = jnp.where(top, sol[0:1], sol[NR - 1 : NR])
        now = sol * (one - (m_row * wide(w_row, NR) + m_lane * wide(w_we[:, 64 + k : 65 + k], NR)))
        a_out[k] = now
        v = nu[k] * m * now
        to_up[pl.ds(k, 1), :] = v[0:1]
        to_down[pl.ds(k, 1), :] = v[NR - 1 : NR]
        acc_l = jnp.where(lane24 == k, pltpu.roll(v, k, 1) if k else v, acc_l)
        acc_r = jnp.where(lane24 == k, pltpu.roll(v, k + 1, 1), acc_r)
    v_left[...] = acc_l
    v_right[...] = acc_r
    for i in (*range(K, 56), *range(56 + K, 112)):
        g_s[pl.ds(i, 1), :] = jnp.zeros((1, L), F32)
    sums = row_sums(g_s[...], x)
    sums = pltpu.roll(sums, lax.rem(L - first_lane(t), L), 1)
    sums = sums[0:56] + pltpu.roll(sums[56:112], 64, 1)
    sums = jnp.where((g == 0) | (g == GY - 1), sums, 0.0)
    for to in (to_up, to_down):
        to[K:56, :] = jnp.zeros((56 - K, L), F32)
        to[56:112, :] = sums

    side[...] = jnp.zeros(side.shape, F32)

    @pl.when((x == 0) | (x == GX - 1))
    def _():
        acc = zero
        for k in range(K):
            acc = jnp.where(lane24 == k, pltpu.roll(a[k], lax.rem(k + is31, L), 1), acc)
            acc = jnp.where(lane24 == 64 + k, pltpu.roll(y_s[k], lax.rem(64 + k + is31, L), 1), acc)
        w24_s[...] = w_we * acc
        side[0:8, :] = w24_s[pl.ds(0, 8, 3), :] + w24_s[pl.ds(1, 8, 3), :] + w24_s[pl.ds(2, 8, 3), :]
        side[8:16, :] = mine


def inner_kernel(
    o_row, o_col, a, nu, mask, kappa, across, down, up, third, pay, row_k, q,
    a_out, q_out,
    e_s, g_s, t_s, up_s, tile_s, fact_s, sem,
):
    g, x, oy, ox = place(o_row, o_col)
    row_ok, row = ring_row(g, x, oy)
    tile = pl.multiple_of(8 * (row // 8), 8)
    at = pl.ds(tile, 8)

    def tile_copy():
        return pltpu.make_async_copy(q.at[:, at, :], tile_s, sem)

    @pl.when(row_ok)
    def _():
        tile_copy().start()

    m = mask[...].astype(F32)
    row24, lane24 = iota((NR, L), 0), iota((NR, L), 1)

    def unpacked(p):
        return jnp.concatenate([p, pltpu.roll(p, 64, 1)], 0)

    hl = jnp.where(x > 0, unpacked(across[jnp.maximum(x - 1, 0), K:62]), 0.0)
    hr = jnp.where(x < GX - 1, unpacked(across[jnp.minimum(x + 1, GX - 1), K:62]), 0.0)
    up_s[...] = third[...] + jnp.where((g == 4) | (g == 5), 0.0, down[0:K, :])
    zero = jnp.zeros((NR, L), F32)
    c_prev, e_prev, y = zero, zero, zero
    for k in range(K):
        now = a[k]
        v = nu[k] * m * now
        above = jnp.where(row24 == 0, wide(up_s[pl.ds(k, 1), :], NR), pltpu.roll(v, 1, 0))
        below = jnp.where(row24 == NR - 1, wide(up[pl.ds(k, 1), :], NR), pltpu.roll(v, NR - 1, 0))
        left = jnp.where(lane24 == 0, wide(hl[:, k : k + 1], NR), pltpu.roll(v, 1, 1))
        right = jnp.where(lane24 == L - 1, wide(hr[:, k : k + 1], NR), pltpu.roll(v, L - 1, 1))
        b = m * (now + (above + below + left + right - 4.0 * v))
        c = kappa[0, k]
        r = 1.0 / (1.0 + c + c_prev * (1.0 - e_prev))
        e = c * r
        y = (b + c_prev * y) * r
        e_s[k] = e
        a_out[k] = y
        c_prev, e_prev = c, e
    for k in range(K - 2, -1, -1):
        y = a_out[k] + e_s[k] * y
        a_out[k] = y

    @pl.when(row_ok)
    def _():
        sig = ox - COL0
        turn = lax.rem(sig, L)
        low = iota((56, L), 1) < 64

        def come(base):
            first = jnp.zeros((56, L), F32)
            second = jnp.zeros((56, L), F32)
            for t in range(3):
                j = 3 * base + t
                got = jnp.where((j >= 0) & (j < GX), across[jnp.clip(j, 0, GX - 1), 0:56], 0.0)
                one = jnp.where(low, got, 0.0)
                two = jnp.where(low, pltpu.roll(got, 64, 1), 0.0)
                start = (0, 42, 85)[t]
                first = first + (pltpu.roll(one, start, 1) if t else one)
                second = second + (pltpu.roll(two, start, 1) if t else two)
            return first, second

        def on_parent(own, prev):
            return jnp.where(iota(own.shape, 1) >= sig, pltpu.roll(own, turn, 1), pltpu.roll(prev, turn, 1))

        own, prev = come(x - WEST), come(x - WEST - 1)
        g_s[0:56, :] = on_parent(own[0], prev[0]) * pay[0:56, :]
        g_s[K : 2 * K, :] = on_parent(own[1], prev[1])[0:K] * pay[K : 2 * K, :]
        here = iota((8, L), 0) == row - tile
        zero = jnp.zeros((8, L), F32)
        for step in (1, 0):
            c_prev, e_prev, y = zero, zero, zero
            for k in range(K):
                c = row_k[step, k]
                r = 1.0 / (1.0 + c + c_prev * (1.0 - e_prev))
                e = c * r
                fact_s[k] = e
                term = jnp.where(here, wide(g_s[pl.ds(k if step else K + k, 1), :], 8), 0.0)
                y = ((term if step else term + t_s[k]) + c_prev * y) * r
                t_s[k] = y
                c_prev, e_prev = c, e
            for k in range(K - 2, -1, -1):
                y = t_s[k] + fact_s[k] * y
                t_s[k] = y
        tile_copy().wait()
        t_s[...] = t_s[...] + tile_s[...]
        back = pltpu.make_async_copy(t_s, q_out.at[:, at, :], sem)
        back.start()
        back.wait()


def outer_kernel(o_row, o_col, sides, col_c, col_r, q, q_out, s_w, s_g, panel_s, local_s, d_s, q_s, sems):
    g, x, oy, ox = place(o_row, o_col)
    is_west, is_east, spot = side_lane(x, ox)
    side_ok = (is_west | is_east) & (g >= SOUTH) & (g < GY - 1)

    def whole_copy():
        return pltpu.make_async_copy(q, q_s, sems.at[0])

    @pl.when(side_ok)
    def _():
        whole_copy().start()

    def panels(first):
        return jnp.concatenate([sides[i, 16 * e + first : 16 * e + first + 8, :] for e in (0, 1) for i in range(GY)], 0)

    grads = panels(0)
    flip_g = grads.T
    flip_w = panels(8).T
    for i, s in enumerate((1, 0)):
        for e in (0, 1):
            s_g[s, :, e, :] = flip_g[64 * i : 64 * i + K, SR * e : SR * e + SR]
            s_w[s, :, e, :] = flip_w[64 * i : 64 * i + K, SR * e : SR * e + SR]

    @pl.when(side_ok)
    def _():
        panel_s[...] = jnp.zeros(panel_s.shape, F32)
        panel_s[SR : 2 * SR, :] = jnp.where(is_west, grads[0:SR], grads[SR : 2 * SR])
        start = PR * g - oy + SR
        for r in range(PR):
            local_s[pl.ds(r, 1), :] = panel_s[pl.ds(start + r, 1), :]
        here = iota((PR, L), 1) == spot
        lane = iota((PR, L), 1)
        cs, rs = col_c[...], col_r[...]
        above = jnp.where((lane == 0) | (lane == 64), 0.0, pltpu.roll(cs, 1, 1)) * rs
        below = cs * rs
        own = local_s[...] * rs

        def column(values, i):
            return wide(values[:, i : i + 1], PR)

        zero = jnp.zeros((PR, L), F32)
        for step, first in ((1, 0), (0, 64)):
            y = zero
            for k in range(K):
                term = column(own, first + k)
                if step == 0:
                    term = term + d_s[k] * column(rs, first + k)
                y = term + column(above, first + k) * y
                d_s[k] = y
            if step == 1:
                for k in range(K - 2, -1, -1):
                    y = d_s[k] + column(below, first + k) * y
                    d_s[k] = y
        whole_copy().wait()
        d_s[K - 1] = jnp.where(here, y, 0.0) + q_s[K - 1]
        copies = []
        for k in range(K - 2, -1, -1):
            y = d_s[k] + column(below, 64 + k) * y
            d_s[k] = jnp.where(here, y, 0.0) + q_s[k]
            if k % 10 == 0:
                part = pl.ds(k, 10)
                copies.append(pltpu.make_async_copy(d_s.at[part], q_out.at[part], sems.at[1 + k // 10]))
                copies[-1].start()
        for copy in copies:
            copy.wait()


def shape(*dims):
    return jax.ShapeDtypeStruct(dims, F32)


def at(g, x):
    return g * GX + x


def moved(value, pairs):
    return lax.ppermute(value, ("gy", "gx"), pairs)


def shifted(value, axis, count, step):
    pairs = [(i, i + step) for i in range(count) if 0 <= i + step < count]
    return lax.ppermute(value, axis, pairs)


def panel_routes():
    routes = []
    for t in TURNS:
        pairs = []
        for p in range(WEST, WEST + 12):
            j = 3 * (p - WEST) + t
            if 0 <= j < GX:
                pairs += [(at(4, p), at(0, j)), (at(5, p), at(7, j))]
        routes.append(pairs)
    for p, e, first in ((WEST, 0, 1), (WEST + 10, GX - 1, 3), (WEST + 11, GX - 1, 5)):
        for k in range(GY - 1):
            routes[(first + k) % 7].append((at(6, p), at(k, e)))
    for p, n in SEVENTH:
        routes[n].append((at(5, p), at(7, 0 if p == WEST else GX - 1)))
    return routes


def on_device(nest_adjoint, nest_kappa, nest_nu, land_mask, parent_adjoint, parent_kappa, parent_traj, offset_row, offset_col):
    here = (offset_row, offset_col)
    to_up, to_down, v_left, v_right, pay = pl.pallas_call(
        edge_kernel,
        out_shape=(shape(56, L), shape(120, L), shape(NR, L), shape(NR, L), shape(168, L)),
        in_specs=[SM] * 2 + [VM] * 3 + [HB],
        out_specs=(VM,) * 5,
        scratch_shapes=[
            pltpu.VMEM((2, K, 8, L), F32), pltpu.VMEM((2, K, PR, L), F32), pltpu.VMEM((256, L), F32),
            pltpu.SemaphoreType.DMA((3,)),
        ],
        compiler_params=grant(60),
        name="edge",
    )(*here, nest_adjoint, nest_nu, land_mask, parent_traj)
    down = shifted(to_down, "gy", GY, 1)
    up = shifted(to_up, "gy", GY, -1)
    ring = range(WEST, WEST + 12)
    skip = moved(
        pay, [(at(6, p), at(5, p)) for p in ring] + [(at(4, p), at(6, p)) for p in (WEST, WEST + 10, WEST + 11)]
    )
    h_left = shifted(v_right, "gx", GX, 1)
    h_right = shifted(v_left, "gx", GX, -1)
    mixed = pl.pallas_call(
        mix_kernel,
        out_shape=(shape(SR, L),) * 7,
        in_specs=[SM] + [VM] * 3 + [ANY] * 2,
        out_specs=(VM,) * 7,
        compiler_params=grant(4),
        name="mix",
    )(offset_col, pay, down, skip, h_left, h_right)
    parts = [moved(message, pairs) for message, pairs in zip(mixed, panel_routes())]
    nest, parent = shape(K, NR, L), shape(K, PR, L)
    base, row_k, col_c, col_r = pl.pallas_call(
        base_kernel,
        out_shape=(parent, shape(2, K, 8, L), shape(PR, L), shape(PR, L)),
        in_specs=[SM] * 2 + [VM] * 2 + [ANY],
        out_specs=(VM,) * 4,
        scratch_shapes=[pltpu.VMEM((K, PR, L), F32), pltpu.VMEM((2, K, PR, L), F32)],
        compiler_params=grant(16),
        cost_estimate=pl.CostEstimate(flops=10000000, bytes_accessed=12000000, transcendentals=0),
        name="base",
    )(*here, parent_adjoint, parent_kappa, mixed[6])

    state, to_up, to_down, v_left, v_right, side = pl.pallas_call(
        nest_kernel,
        out_shape=(nest, shape(112, L), shape(112, L), shape(NR, L), shape(NR, L), shape(16, L)),
        in_specs=[SM] * 2 + [VM] * 15 + [ANY],
        out_specs=(VM,) * 6,
        scratch_shapes=[
            pltpu.VMEM((K, NR, L), F32), pltpu.VMEM((K, NR, L), F32), pltpu.VMEM((112, L), F32), pltpu.VMEM((K, L), F32),
            pltpu.VMEM((K, L), F32), pltpu.VMEM((112, L), F32), pltpu.VMEM((SR, L), F32),
            pltpu.VMEM((NR, L), F32),
        ],
        compiler_params=grant(12),
        name="nest",
    )(*here, nest_adjoint, nest_nu, land_mask, nest_kappa, down, up, h_left, h_right, *parts, col_c)

    rows = ((0, 4), (7, 5), (1, 2), (2, 3), (5, 6), (6, 7))
    down = moved(to_down, [(at(i, j), at(k, j)) for i, k in rows for j in range(GX)])
    up = shifted(to_up, "gy", GY, -1)
    third = moved(to_down[0:K], [(at(i, j), at(i + 1, j)) for i in (0, 3, 4) for j in range(GX)])
    across = pl.pallas_call(
        spread_kernel,
        out_shape=shape(GX, 80, L),
        in_specs=[VM] * 5 + [ANY],
        out_specs=VM,
        scratch_shapes=[pltpu.VMEM((80, L), F32)],
        compiler_params=grant(4),
        name="spread",
    )(side, v_left, v_right, down, up, third)
    across = lax.all_to_all(across, "gx", 0, 0)
    sides = pl.pallas_call(
        turn_kernel, out_shape=shape(GY, 32, L), in_specs=[VM], out_specs=VM, compiler_params=grant(4), name="turn"
    )(across)
    sides = lax.all_to_all(sides, "gy", 0, 0)

    state, base = pl.pallas_call(
        inner_kernel,
        out_shape=(nest, parent),
        in_specs=[SM] * 2 + [VM] * 10 + [HB],
        out_specs=(VM, HB),
        scratch_shapes=[
            pltpu.VMEM((K, NR, L), F32), pltpu.VMEM((104, L), F32), pltpu.VMEM((K, 8, L), F32), pltpu.VMEM((K, L), F32),
            pltpu.VMEM((K, 8, L), F32), pltpu.VMEM((K, 8, L), F32), pltpu.SemaphoreType.DMA,
        ],
        input_output_aliases={12: 1},
        compiler_params=grant(14),
        name="inner",
    )(*here, state, nest_nu, land_mask, nest_kappa, across, down, up, third, pay, row_k, base)
    base, side_weights, side_gradients = pl.pallas_call(
        outer_kernel,
        out_shape=(parent, shape(2, K, 2, SR), shape(2, K, 2, SR)),
        in_specs=[SM] * 2 + [VM] * 3 + [HB],
        out_specs=(HB, VM, VM),
        scratch_shapes=[
            pltpu.VMEM((256, L), F32), pltpu.VMEM((PR, L), F32), pltpu.VMEM((K, PR, L), F32), pltpu.VMEM((K, PR, L), F32),
            pltpu.SemaphoreType.DMA((6,)),
        ],
        input_output_aliases={5: 0},
        compiler_params=grant(12),
        name="outer",
    )(*here, sides, col_c, col_r, base)
    return state, base, side_weights, side_gradients


def solution(mesh):
    in_specs = (
        P(None, "gy", "gx"),
        P(None, None, "gy", "gx"),
        P(None, "gy", "gx"),
        P("gy", "gx"),
        P(None, "gy", "gx"),
        P(None, None, "gy", "gx"),
        P(None, None, "gy", "gx"),
        P(),
        P(),
    )
    out_specs = (P(None, "gy", "gx"), P(None, "gy", "gx"), P(), P())
    return jax.shard_map(on_device, mesh=mesh, in_specs=in_specs, out_specs=out_specs, check_vma=False)
```

```python
import jax
import jax.numpy as jnp
from jax import lax
from jax.experimental import pallas as pl
from jax.experimental.pallas import tpu as pltpu
from jax.sharding import PartitionSpec as P

R = 3
K = 50
NR = 24
PR = 48
L = 128
GY = 8
GX = 32
SR = 64
ROW0 = 192
COL0 = 2048
SOUTH = 4
WEST = 16
SPAN = 1366
F32 = jnp.float32
VM = pl.BlockSpec(memory_space=pltpu.VMEM)
SM = pl.BlockSpec(memory_space=pltpu.SMEM)
HB = pl.BlockSpec(memory_space=pltpu.HBM)
ANY = pl.BlockSpec(memory_space=pl.ANY)


def grant(mib):
    return pltpu.CompilerParams(vmem_limit_bytes=mib * 1024 * 1024)


TURNS = (0, 1, 2, -3, -2, -1, -4)
SEVENTH = ((WEST, 4), (WEST + 10, 2), (WEST + 11, 0))


def side_round(i, g):
    return jnp.where(g == GY - 1, SEVENTH[i][1], lax.rem((1, 3, 5)[i] + g, 7))


def exact(left, right):
    return lax.dot_general(
        left, right, (((1,), (0,)), ((), ())), precision=lax.Precision.HIGHEST, preferred_element_type=F32
    )


def exact_t(left, right):
    return lax.dot_general(
        left, right, (((1,), (1,)), ((), ())), precision=lax.Precision.HIGHEST, preferred_element_type=F32
    )


def iota(shape, dim):
    return lax.broadcasted_iota(jnp.int32, shape, dim)


def wide(col, rows):
    return jnp.broadcast_to(col, (rows, L))


def place(row, col):
    return lax.axis_index("gy"), lax.axis_index("gx"), row[0], col[0]


def to_first(values, i):
    return pltpu.roll(values, L - i, 1) if i else values


def to_last(values, i):
    return pltpu.roll(values, L - 1 - i, 1) if i < L - 1 else values


def side_lane(x, ox):
    west = ox - 1 - L * x
    east = ox + SPAN - L * x
    is_west = (west >= 0) & (west < L)
    is_east = (east >= 0) & (east < L)
    return is_west, is_east, jnp.where(is_west, west, east)


def ring_row(g, x, oy):
    row = jnp.where(g == SOUTH, oy - 1, oy + SR) - PR * g
    ok = (row >= 0) & (row < PR) & (g >= SOUTH) & (g < GY - 1) & (x >= WEST) & (x < WEST + 12)
    return ok, row


def threes(x, shape, dim):
    cell = L * lax.rem(x, 3) + iota(shape, dim)
    first = 3 * iota(shape, 1 - dim)
    return ((first <= cell) & (cell < first + 3)).astype(F32)


def row_sums(rows, x):
    col = x * L + iota(rows.shape, 1)
    return exact(jnp.where((col > 0) & (col < GX * L - 1), rows, 0.0), threes(x, (L, L), 0))


def edge_kernel(o_row, o_col, a, nu, mask, traj, to_up, to_down, v_left, v_right, pay, row_s, col_s, buf, sems):
    g, x, oy, ox = place(o_row, o_col)
    row_ok, row = ring_row(g, x, oy)
    is_west, is_east, spot = side_lane(x, ox)
    side_ok = (is_west | is_east) & (g >= SOUTH) & (g < GY - 1)
    tile = pl.multiple_of(8 * (row // 8), 8)

    def row_copy():
        return pltpu.make_async_copy(traj.at[:, :, pl.ds(tile, 8), :], row_s, sems.at[2])

    def col_copy(s):
        return pltpu.make_async_copy(traj.at[s], col_s.at[s], sems.at[s])

    @pl.when(side_ok)
    def _():
        col_copy(1).start()
        col_copy(0).start()

    @pl.when(row_ok)
    def _():
        row_copy().start()

    m = mask[...].astype(F32)
    lane = iota((NR, L), 1)
    acc_l = jnp.zeros((NR, L), F32)
    acc_r = jnp.zeros((NR, L), F32)
    for k in range(K):
        v = nu[k] * m * a[k]
        to_up[pl.ds(k, 1), :] = v[0:1]
        to_down[pl.ds(k, 1), :] = v[NR - 1 : NR]
        acc_l = jnp.where(lane == k, pltpu.roll(v, k, 1) if k else v, acc_l)
        acc_r = jnp.where(lane == k, pltpu.roll(v, k + 1, 1), acc_r)
    v_left[...] = acc_l
    v_right[...] = acc_r
    pay[...] = jnp.zeros(pay.shape, F32)

    @pl.when(row_ok)
    def _():
        row_copy().wait()
        for i, s in enumerate((1, 0)):
            for k in range(K):
                pay[pl.ds(K * i + k, 1), :] = jax.nn.sigmoid(row_s[s, k, pl.ds(row - tile, 1), :])

    @pl.when(side_ok)
    def _():
        plane = iota((PR, L), 1)
        acc = jnp.zeros((PR, L), F32)
        for i, s in enumerate((1, 0)):
            col_copy(s).wait()
            for k in range(K):
                to = 64 * i + k
                acc = jnp.where(plane == to, pltpu.roll(col_s[s, k], lax.rem(to - spot + L, L), 1), acc)
        used = (plane < K) | ((plane >= 64) & (plane < 64 + K))
        buf[...] = jnp.zeros(buf.shape, F32)
        start = PR * g - oy + SR
        weights = jnp.where(used, jax.nn.sigmoid(acc), 0.0)
        for r in range(PR):
            buf[pl.ds(start + r, 1), :] = weights[r : r + 1]
        pay[104:168, :] = buf[SR : 2 * SR, :]

    for to in (to_up, to_down):
        to[K:56, :] = jnp.zeros((56 - K, L), F32)
    to_down[56:120, :] = pay[104:168, :]


def mix_kernel(o_col, pay, down, skip, after_left, after_right, *outs):
    g, x = lax.axis_index("gy"), lax.axis_index("gx")
    sig = o_col[0] - COL0
    own = pay[0:104, :] + jnp.where(g == 5, skip[0:104, :], 0.0)
    sides = pay[104:168, :] + down[56:120, :] + skip[104:168, :]
    lane = iota((K, L), 1)
    spare = jnp.zeros((64 - K, L), F32)
    for i, (t, out) in enumerate(zip(TURNS, outs)):
        begin = (0, 42, 85)[t % 3] - 1 + L * (t // 3) + sig
        turn = lax.rem(4 * L - begin, L)
        cell = begin + lane
        one = jnp.where((lane < 48) & (cell >= 0) & (cell < L), pltpu.roll(own[0:K], turn, 1), 0.0)
        cell = cell - 64
        two = jnp.where(
            (lane >= 64) & (lane < 112) & (cell >= 0) & (cell < L), pltpu.roll(own[K : 2 * K], lax.rem(turn + 64, L), 1), 0.0
        )
        part = jnp.concatenate([one + two, spare], 0)
        extra = g == 6
        for p, n in SEVENTH:
            extra = extra | ((g == 5) & (x == p) & (n == i))
        out[...] = jnp.where(extra, sides, part)


def base_kernel(o_row, o_col, q, pkappa, after, q_out, row_k, col_c, col_r, e_s, r_s):
    g, x, oy, ox = place(o_row, o_col)
    zero = jnp.zeros((PR, L), F32)
    src = q
    for step in (1, 0):
        c_prev, e_prev, y = zero, zero, zero
        for k in range(K):
            c = pkappa[step, k]
            r = 1.0 / (1.0 + c + c_prev * (1.0 - e_prev))
            e = c * r
            e_s[k] = e
            r_s[step, k] = r
            y = (src[k] + c_prev * y) * r
            q_out[k] = y
            c_prev, e_prev = c, e
        for k in range(K - 2, -1, -1):
            y = q_out[k] + e_s[k] * y
            q_out[k] = y
        src = q_out
    row_ok, row = ring_row(g, x, oy)
    is_west, is_east, spot = side_lane(x, ox)

    @pl.when(row_ok)
    def _():
        row_k[...] = pkappa[:, :, pl.ds(pl.multiple_of(8 * (row // 8), 8), 8), :]

    @pl.when(is_west | is_east)
    def _():
        lane = iota((PR, L), 1)
        for values, out in ((pkappa, col_c), (r_s, col_r)):
            acc = zero
            for i, s in enumerate((1, 0)):
                for k in range(K):
                    to = 64 * i + k
                    acc = jnp.where(lane == to, pltpu.roll(values[s, k], lax.rem(to - spot + L, L), 1), acc)
            out[...] = acc


def spread_kernel(side, v_left, v_right, down, up, after, out, one_s):
    x = lax.axis_index("gx")

    def packed(v):
        return v[0:12] + pltpu.roll(v[12:24], 64, 1)

    to_left, to_right = packed(v_left[...]), packed(v_right[...])
    one_s[0:K, :] = down[56 : 56 + K, :] + up[56 : 56 + K, :]
    one_s[K:62, :] = jnp.zeros((62 - K, L), F32)
    one_s[62:78, :] = side[...]
    one_s[78:80, :] = jnp.zeros((2, L), F32)
    every = one_s[...]
    for i in range(GX):
        out[i] = every

    @pl.when(x > 0)
    def _():
        out[jnp.maximum(x - 1, 0), K:62, :] = to_left

    @pl.when(x < GX - 1)
    def _():
        out[jnp.minimum(x + 1, GX - 1), K:62, :] = to_right


def turn_kernel(across, out):
    west, east = across[0, 62:78], across[GX - 1, 62:78]
    for i in range(GY):
        out[i, 0:16] = west
        out[i, 16:32] = east


def first_lane(t):
    return jnp.where(t == 0, 0, jnp.where(t == 1, 42, 85))


def nest_kernel(
    o_row, o_col, a, nu, mask, kappa, h_up, h_down, h_left, h_right, *rest,
):
    parts = rest[:7]
    a_out, to_up, to_down, v_left, v_right, side, e_s, y_s, w_s, up_s, down_s, g_s, we_s, w24_s = rest[8:]
    g, x, oy, ox = place(o_row, o_col)
    t = lax.rem(x, 3)
    def pick(i):
        got = jnp.where(t == 0, parts[i][...], parts[i + 1][...])
        return jnp.where(t == 2, parts[i + 2][...], got)

    window = (pick(0) + pick(3) + jnp.where(t == 2, parts[6][...], 0.0))[0:56]
    wl = iota((56, L), 1)
    low = wl < 64
    panel = jnp.concatenate([jnp.where(low, window, 0.0), jnp.where(low, pltpu.roll(window, 64, 1), 0.0)], 0)
    shift = first_lane(t) - 1
    si, sc = iota((L, L), 0) + shift, L * t + iota((L, L), 1)
    spread = ((3 * si <= sc) & (sc < 3 * si + 3)).astype(F32)
    c_all = x * L + iota((112, L), 1)
    inner = (c_all > 0) & (c_all < GX * L - 1) & ((g == 0) | (g == GY - 1))
    w_s[...] = jnp.where(inner, exact(panel, spread), 0.0)

    er, el = iota((8, L), 0), iota((8, L), 1)
    want = jnp.where(er == 0, jnp.where(t == 0, 0, 1), jnp.where(er == 1, jnp.where(t == 0, 43, 44), -1))
    ends = exact_t((el == want).astype(F32), panel[0:56])

    row24, lane24 = iota((NR, L), 0), iota((NR, L), 1)
    m_row = (((row24 == 0) & (g == 0)) | ((row24 == NR - 1) & (g == GY - 1))).astype(F32)
    m_lane = (((lane24 == 0) & (x == 0)) | ((lane24 == L - 1) & (x == GX - 1))).astype(F32)
    ends_l = jnp.concatenate([ends[0:1], jnp.zeros((1, L - 56), F32)], 1)
    ends_r = jnp.concatenate([ends[1:2], jnp.zeros((1, L - 56), F32)], 1)
    hl = h_left[...] * (1.0 - m_row * wide(ends_l, NR))
    hr = h_right[...] * (1.0 - m_row * wide(ends_r, NR))

    panel_we = jnp.zeros((SR, L), F32)
    for i, part in enumerate(parts):
        come = ((x == 0) & (side_round(0, g) == i)) | (
            (x == GX - 1) & ((side_round(1, g) == i) | (side_round(2, g) == i))
        )
        panel_we = panel_we + jnp.where(come, part[...], 0.0)
    we_s[...] = panel_we
    mine = we_s[pl.ds(pl.multiple_of(8 * g, 8), 8), :]
    for i in range(8):
        w24_s[3 * i : 3 * i + 3, :] = jnp.broadcast_to(mine[i : i + 1], (3, L))
    w_we = w24_s[...]
    flip = jnp.concatenate([panel_we, jnp.zeros((SR, L), F32)], 0).T[0:56]
    spot = jnp.where(x == 0, 0, L - 1)
    lane56 = iota((56, L), 1)
    edge = (lane56 == spot) & ((x == 0) | (x == GX - 1))
    w_up = jnp.where(edge & (g > 0), pltpu.roll(flip, lax.rem(spot - (8 * g - 1) + L, L), 1), 0.0)
    w_down = jnp.where(edge & (g < GY - 1), pltpu.roll(flip, lax.rem(spot - (8 * g + 8) + L, L), 1), 0.0)
    up_s[...] = h_up[0:K, :] * (1.0 - w_up[0:K])
    down_s[...] = h_down[0:K, :] * (1.0 - w_down[0:K])

    w_edge = jnp.where(x == 0, w_we, pltpu.roll(w_we, L - 1, 1))
    m = mask[...].astype(F32)
    one = jnp.ones((NR, L), F32)
    zero = jnp.zeros((NR, L), F32)
    c_prev, e_prev, y = zero, zero, zero
    top = g == 0
    side_ok = (x == 0) | (x == GX - 1)

    @pl.when(side_ok)
    def _():
        for k in range(K):
            y_s[k] = a[k] * (one - m_lane * to_first(w_edge, k))

    @pl.when(jnp.logical_not(side_ok))
    def _():
        y_s[...] = a[...]

    is31 = (x == GX - 1).astype(jnp.int32)
    for k in range(K):
        w_row = w_s[pl.ds(k, 1), :]
        raw = y_s[k]
        g_s[pl.ds(k, 1), :] = jnp.where(top, raw[0:1], raw[NR - 1 : NR])
        now = raw * (one - m_row * wide(w_row, NR))
        v = nu[k] * m * now
        above = jnp.where(row24 == 0, wide(up_s[pl.ds(k, 1), :], NR), pltpu.roll(v, 1, 0))
        below = jnp.where(row24 == NR - 1, wide(down_s[pl.ds(k, 1), :], NR), pltpu.roll(v, NR - 1, 0))
        left = jnp.where(lane24 == 0, to_first(hl, k), pltpu.roll(v, 1, 1))
        right = jnp.where(lane24 == L - 1, to_last(hr, k), pltpu.roll(v, L - 1, 1))
        b = m * (now + (above + below + left + right - 4.0 * v))
        c = kappa[1, k]
        r = 1.0 / (1.0 + c + c_prev * (1.0 - e_prev))
        e = c * r
        y = (b + c_prev * y) * r
        e_s[k] = e
        y_s[k] = y
        c_prev, e_prev = c, e
    sol = zero
    acc_l, acc_r = zero, zero
    for k in range(K - 1, -1, -1):
        sol = y_s[k] + e_s[k] * sol if k < K - 1 else y_s[k]
        y_s[k] = sol
    for k in range(K):
        sol = y_s[k]
        g_s[pl.ds(56 + k, 1), :] = jnp.where(top, sol[0:1], sol[NR - 1 : NR])
        a_out[k] = sol * (one - m_row * wide(w_s[pl.ds(56 + k, 1), :], NR))

    @pl.when(side_ok)
    def _():
        for k in range(K):
            a_out[k] = a_out[k] * (one - m_lane * to_first(w_edge, 64 + k))

    for k in range(K):
        v = nu[k] * m * a_out[k]
        to_up[pl.ds(k, 1), :] = v[0:1]
        to_down[pl.ds(k, 1), :] = v[NR - 1 : NR]
        acc_l = jnp.where(lane24 == k, pltpu.roll(v, k, 1) if k else v, acc_l)
        acc_r = jnp.where(lane24 == k, pltpu.roll(v, k + 1, 1), acc_r)
    v_left[...] = acc_l
    v_right[...] = acc_r
    for i in (*range(K, 56), *range(56 + K, 112)):
        g_s[pl.ds(i, 1), :] = jnp.zeros((1, L), F32)
    sums = row_sums(g_s[...], x)
    sums = pltpu.roll(sums, lax.rem(L - first_lane(t), L), 1)
    sums = sums[0:56] + pltpu.roll(sums[56:112], 64, 1)
    sums = jnp.where((g == 0) | (g == GY - 1), sums, 0.0)
    for to in (to_up, to_down):
        to[K:56, :] = jnp.zeros((56 - K, L), F32)
        to[56:112, :] = sums

    side[...] = jnp.zeros(side.shape, F32)

    @pl.when((x == 0) | (x == GX - 1))
    def _():
        acc = zero
        for k in range(K):
            acc = jnp.where(lane24 == k, pltpu.roll(a[k], lax.rem(k + is31, L), 1), acc)
            acc = jnp.where(lane24 == 64 + k, pltpu.roll(y_s[k], lax.rem(64 + k + is31, L), 1), acc)
        w24_s[...] = w_we * acc
        side[0:8, :] = w24_s[pl.ds(0, 8, 3), :] + w24_s[pl.ds(1, 8, 3), :] + w24_s[pl.ds(2, 8, 3), :]
        side[8:16, :] = mine


def inner_kernel(
    o_row, o_col, a, nu, mask, kappa, across, down, up, third, pay, row_k, q,
    a_out, q_out,
    e_s, g_s, t_s, up_s, tile_s, fact_s, sem,
):
    g, x, oy, ox = place(o_row, o_col)
    row_ok, row = ring_row(g, x, oy)
    tile = pl.multiple_of(8 * (row // 8), 8)
    at = pl.ds(tile, 8)

    def tile_copy():
        return pltpu.make_async_copy(q.at[:, at, :], tile_s, sem)

    @pl.when(row_ok)
    def _():
        tile_copy().start()

    m = mask[...].astype(F32)
    row24, lane24 = iota((NR, L), 0), iota((NR, L), 1)

    def unpacked(p):
        return jnp.concatenate([p, pltpu.roll(p, 64, 1)], 0)

    hl = jnp.where(x > 0, unpacked(across[jnp.maximum(x - 1, 0), K:62]), 0.0)
    hr = jnp.where(x < GX - 1, unpacked(across[jnp.minimum(x + 1, GX - 1), K:62]), 0.0)
    up_s[...] = third[...] + jnp.where((g == 4) | (g == 5), 0.0, down[0:K, :])
    zero = jnp.zeros((NR, L), F32)
    c_prev, e_prev, y = zero, zero, zero
    for k in range(K):
        now = a[k]
        v = nu[k] * m * now
        above = jnp.where(row24 == 0, wide(up_s[pl.ds(k, 1), :], NR), pltpu.roll(v, 1, 0))
        below = jnp.where(row24 == NR - 1, wide(up[pl.ds(k, 1), :], NR), pltpu.roll(v, NR - 1, 0))
        left = jnp.where(lane24 == 0, to_first(hl, k), pltpu.roll(v, 1, 1))
        right = jnp.where(lane24 == L - 1, to_last(hr, k), pltpu.roll(v, L - 1, 1))
        b = m * (now + (above + below + left + right - 4.0 * v))
        c = kappa[0, k]
        r = 1.0 / (1.0 + c + c_prev * (1.0 - e_prev))
        e = c * r
        y = (b + c_prev * y) * r
        e_s[k] = e
        a_out[k] = y
        c_prev, e_prev = c, e
    for k in range(K - 2, -1, -1):
        y = a_out[k] + e_s[k] * y
        a_out[k] = y

    @pl.when(row_ok)
    def _():
        sig = ox - COL0
        turn = lax.rem(sig, L)
        low = iota((56, L), 1) < 64

        def come(base):
            first = jnp.zeros((56, L), F32)
            second = jnp.zeros((56, L), F32)
            for t in range(3):
                j = 3 * base + t
                got = jnp.where((j >= 0) & (j < GX), across[jnp.clip(j, 0, GX - 1), 0:56], 0.0)
                one = jnp.where(low, got, 0.0)
                two = jnp.where(low, pltpu.roll(got, 64, 1), 0.0)
                start = (0, 42, 85)[t]
                first = first + (pltpu.roll(one, start, 1) if t else one)
                second = second + (pltpu.roll(two, start, 1) if t else two)
            return first, second

        def on_parent(own, prev):
            return jnp.where(iota(own.shape, 1) >= sig, pltpu.roll(own, turn, 1), pltpu.roll(prev, turn, 1))

        own, prev = come(x - WEST), come(x - WEST - 1)
        g_s[0:56, :] = on_parent(own[0], prev[0]) * pay[0:56, :]
        g_s[K : 2 * K, :] = on_parent(own[1], prev[1])[0:K] * pay[K : 2 * K, :]
        here = iota((8, L), 0) == row - tile
        zero = jnp.zeros((8, L), F32)
        for step in (1, 0):
            c_prev, e_prev, y = zero, zero, zero
            for k in range(K):
                c = row_k[step, k]
                r = 1.0 / (1.0 + c + c_prev * (1.0 - e_prev))
                e = c * r
                fact_s[k] = e
                term = jnp.where(here, wide(g_s[pl.ds(k if step else K + k, 1), :], 8), 0.0)
                y = ((term if step else term + t_s[k]) + c_prev * y) * r
                t_s[k] = y
                c_prev, e_prev = c, e
            for k in range(K - 2, -1, -1):
                y = t_s[k] + fact_s[k] * y
                t_s[k] = y
        tile_copy().wait()
        t_s[...] = t_s[...] + tile_s[...]
        back = pltpu.make_async_copy(t_s, q_out.at[:, at, :], sem)
        back.start()
        back.wait()


def outer_kernel(o_row, o_col, sides, col_c, col_r, q, q_out, s_w, s_g, panel_s, local_s, d_s, q_s, sems):
    g, x, oy, ox = place(o_row, o_col)
    is_west, is_east, spot = side_lane(x, ox)
    side_ok = (is_west | is_east) & (g >= SOUTH) & (g < GY - 1)

    def whole_copy():
        return pltpu.make_async_copy(q, q_s, sems.at[0])

    @pl.when(side_ok)
    def _():
        whole_copy().start()

    def panels(first):
        return jnp.concatenate([sides[i, 16 * e + first : 16 * e + first + 8, :] for e in (0, 1) for i in range(GY)], 0)

    grads = panels(0)
    flip_g = grads.T
    flip_w = panels(8).T
    for i, s in enumerate((1, 0)):
        for e in (0, 1):
            s_g[s, :, e, :] = flip_g[64 * i : 64 * i + K, SR * e : SR * e + SR]
            s_w[s, :, e, :] = flip_w[64 * i : 64 * i + K, SR * e : SR * e + SR]

    @pl.when(side_ok)
    def _():
        panel_s[...] = jnp.zeros(panel_s.shape, F32)
        panel_s[SR : 2 * SR, :] = jnp.where(is_west, grads[0:SR], grads[SR : 2 * SR])
        start = PR * g - oy + SR
        for r in range(PR):
            local_s[pl.ds(r, 1), :] = panel_s[pl.ds(start + r, 1), :]
        here = iota((PR, L), 1) == spot
        lane = iota((PR, L), 1)
        own = local_s[...]
        cs, rs = col_c[...], col_r[...]
        above = jnp.where((lane == 0) | (lane == 64), 0.0, pltpu.roll(cs, 1, 1)) * rs
        below = cs * rs
        own = own * rs
        own, above, below, rs = (pltpu.roll(v, spot, 1) for v in (own, above, below, rs))

        def column(values, i):
            return to_first(values, i)

        zero = jnp.zeros((PR, L), F32)
        for step, first in ((1, 0), (0, 64)):
            y = zero
            for k in range(K):
                term = column(own, first + k)
                if step == 0:
                    term = term + d_s[k] * column(rs, first + k)
                y = term + column(above, first + k) * y
                d_s[k] = y
            if step == 1:
                for k in range(K - 2, -1, -1):
                    y = d_s[k] + column(below, first + k) * y
                    d_s[k] = y
        whole_copy().wait()
        d_s[K - 1] = jnp.where(here, y, 0.0) + q_s[K - 1]
        copies = []
        for k in range(K - 2, -1, -1):
            y = d_s[k] + column(below, 64 + k) * y
            d_s[k] = jnp.where(here, y, 0.0) + q_s[k]
            if k % 10 == 0:
                part = pl.ds(k, 10)
                copies.append(pltpu.make_async_copy(d_s.at[part], q_out.at[part], sems.at[1 + k // 10]))
                copies[-1].start()
        for copy in copies:
            copy.wait()


def shape(*dims):
    return jax.ShapeDtypeStruct(dims, F32)


def at(g, x):
    return g * GX + x


def moved(value, pairs):
    return lax.ppermute(value, ("gy", "gx"), pairs)


def shifted(value, axis, count, step):
    pairs = [(i, i + step) for i in range(count) if 0 <= i + step < count]
    return lax.ppermute(value, axis, pairs)


def panel_routes():
    routes = []
    for t in TURNS:
        pairs = []
        for p in range(WEST, WEST + 12):
            j = 3 * (p - WEST) + t
            if 0 <= j < GX:
                pairs += [(at(4, p), at(0, j)), (at(5, p), at(7, j))]
        routes.append(pairs)
    for p, e, first in ((WEST, 0, 1), (WEST + 10, GX - 1, 3), (WEST + 11, GX - 1, 5)):
        for k in range(GY - 1):
            routes[(first + k) % 7].append((at(6, p), at(k, e)))
    for p, n in SEVENTH:
        routes[n].append((at(5, p), at(7, 0 if p == WEST else GX - 1)))
    return routes


def on_device(nest_adjoint, nest_kappa, nest_nu, land_mask, parent_adjoint, parent_kappa, parent_traj, offset_row, offset_col):
    here = (offset_row, offset_col)
    to_up, to_down, v_left, v_right, pay = pl.pallas_call(
        edge_kernel,
        out_shape=(shape(56, L), shape(120, L), shape(NR, L), shape(NR, L), shape(168, L)),
        in_specs=[SM] * 2 + [VM] * 3 + [HB],
        out_specs=(VM,) * 5,
        scratch_shapes=[
            pltpu.VMEM((2, K, 8, L), F32), pltpu.VMEM((2, K, PR, L), F32), pltpu.VMEM((256, L), F32),
            pltpu.SemaphoreType.DMA((3,)),
        ],
        compiler_params=grant(60),
        name="edge",
    )(*here, nest_adjoint, nest_nu, land_mask, parent_traj)
    down = shifted(to_down, "gy", GY, 1)
    up = shifted(to_up, "gy", GY, -1)
    ring = range(WEST, WEST + 12)
    skip = moved(
        pay, [(at(6, p), at(5, p)) for p in ring] + [(at(4, p), at(6, p)) for p in (WEST, WEST + 10, WEST + 11)]
    )
    h_left = shifted(v_right, "gx", GX, 1)
    h_right = shifted(v_left, "gx", GX, -1)
    mixed = pl.pallas_call(
        mix_kernel,
        out_shape=(shape(SR, L),) * 7,
        in_specs=[SM] + [VM] * 3 + [ANY] * 2,
        out_specs=(VM,) * 7,
        compiler_params=grant(4),
        name="mix",
    )(offset_col, pay, down, skip, h_left, h_right)
    parts = [moved(message, pairs) for message, pairs in zip(mixed, panel_routes())]
    nest, parent = shape(K, NR, L), shape(K, PR, L)
    base, row_k, col_c, col_r = pl.pallas_call(
        base_kernel,
        out_shape=(parent, shape(2, K, 8, L), shape(PR, L), shape(PR, L)),
        in_specs=[SM] * 2 + [VM] * 2 + [ANY],
        out_specs=(VM,) * 4,
        scratch_shapes=[pltpu.VMEM((K, PR, L), F32), pltpu.VMEM((2, K, PR, L), F32)],
        compiler_params=grant(16),
        cost_estimate=pl.CostEstimate(flops=10000000, bytes_accessed=12000000, transcendentals=0),
        name="base",
    )(*here, parent_adjoint, parent_kappa, mixed[6])

    state, to_up, to_down, v_left, v_right, side = pl.pallas_call(
        nest_kernel,
        out_shape=(nest, shape(112, L), shape(112, L), shape(NR, L), shape(NR, L), shape(16, L)),
        in_specs=[SM] * 2 + [VM] * 15 + [ANY],
        out_specs=(VM,) * 6,
        scratch_shapes=[
            pltpu.VMEM((K, NR, L), F32), pltpu.VMEM((K, NR, L), F32), pltpu.VMEM((112, L), F32), pltpu.VMEM((K, L), F32),
            pltpu.VMEM((K, L), F32), pltpu.VMEM((112, L), F32), pltpu.VMEM((SR, L), F32),
            pltpu.VMEM((NR, L), F32),
        ],
        compiler_params=grant(12),
        name="nest",
    )(*here, nest_adjoint, nest_nu, land_mask, nest_kappa, down, up, h_left, h_right, *parts, col_c)

    rows = ((0, 4), (7, 5), (1, 2), (2, 3), (5, 6), (6, 7))
    down = moved(to_down, [(at(i, j), at(k, j)) for i, k in rows for j in range(GX)])
    up = shifted(to_up, "gy", GY, -1)
    third = moved(to_down[0:K], [(at(i, j), at(i + 1, j)) for i in (0, 3, 4) for j in range(GX)])
    across = pl.pallas_call(
        spread_kernel,
        out_shape=shape(GX, 80, L),
        in_specs=[VM] * 5 + [ANY],
        out_specs=VM,
        scratch_shapes=[pltpu.VMEM((80, L), F32)],
        compiler_params=grant(4),
        name="spread",
    )(side, v_left, v_right, down, up, third)
    across = lax.all_to_all(across, "gx", 0, 0)
    sides = pl.pallas_call(
        turn_kernel, out_shape=shape(GY, 32, L), in_specs=[VM], out_specs=VM, compiler_params=grant(4), name="turn"
    )(across)
    sides = lax.all_to_all(sides, "gy", 0, 0)

    state, base = pl.pallas_call(
        inner_kernel,
        out_shape=(nest, parent),
        in_specs=[SM] * 2 + [VM] * 10 + [HB],
        out_specs=(VM, HB),
        scratch_shapes=[
            pltpu.VMEM((K, NR, L), F32), pltpu.VMEM((104, L), F32), pltpu.VMEM((K, 8, L), F32), pltpu.VMEM((K, L), F32),
            pltpu.VMEM((K, 8, L), F32), pltpu.VMEM((K, 8, L), F32), pltpu.SemaphoreType.DMA,
        ],
        input_output_aliases={12: 1},
        compiler_params=grant(14),
        name="inner",
    )(*here, state, nest_nu, land_mask, nest_kappa, across, down, up, third, pay, row_k, base)
    base, side_weights, side_gradients = pl.pallas_call(
        outer_kernel,
        out_shape=(parent, shape(2, K, 2, SR), shape(2, K, 2, SR)),
        in_specs=[SM] * 2 + [VM] * 3 + [HB],
        out_specs=(HB, VM, VM),
        scratch_shapes=[
            pltpu.VMEM((256, L), F32), pltpu.VMEM((PR, L), F32), pltpu.VMEM((K, PR, L), F32), pltpu.VMEM((K, PR, L), F32),
            pltpu.SemaphoreType.DMA((6,)),
        ],
        input_output_aliases={5: 0},
        compiler_params=grant(12),
        name="outer",
    )(*here, sides, col_c, col_r, base)
    return state, base, side_weights, side_gradients


def solution(mesh):
    in_specs = (
        P(None, "gy", "gx"),
        P(None, None, "gy", "gx"),
        P(None, "gy", "gx"),
        P("gy", "gx"),
        P(None, "gy", "gx"),
        P(None, None, "gy", "gx"),
        P(None, None, "gy", "gx"),
        P(),
        P(),
    )
    out_specs = (P(None, "gy", "gx"), P(None, "gy", "gx"), P(), P())
    return jax.shard_map(on_device, mesh=mesh, in_specs=in_specs, out_specs=out_specs, check_vma=False)
```

```python
import jax
import jax.numpy as jnp
from jax import lax
from jax.experimental import pallas as pl
from jax.experimental.pallas import tpu as pltpu
from jax.sharding import PartitionSpec as P

R = 3
K = 50
NR = 24
PR = 48
L = 128
GY = 8
GX = 32
SR = 64
ROW0 = 192
COL0 = 2048
SOUTH = 4
WEST = 16
SPAN = 1366
F32 = jnp.float32
VM = pl.BlockSpec(memory_space=pltpu.VMEM)
SM = pl.BlockSpec(memory_space=pltpu.SMEM)
HB = pl.BlockSpec(memory_space=pltpu.HBM)
ANY = pl.BlockSpec(memory_space=pl.ANY)


def grant(mib):
    return pltpu.CompilerParams(vmem_limit_bytes=mib * 1024 * 1024)


TURNS = (0, 1, 2, -3, -2, -1, -4)
SEVENTH = ((WEST, 4), (WEST + 10, 2), (WEST + 11, 0))


def side_round(i, g):
    return jnp.where(g == GY - 1, SEVENTH[i][1], lax.rem((1, 3, 5)[i] + g, 7))


def exact(left, right):
    return lax.dot_general(
        left, right, (((1,), (0,)), ((), ())), precision=lax.Precision.HIGHEST, preferred_element_type=F32
    )


def exact_t(left, right):
    return lax.dot_general(
        left, right, (((1,), (1,)), ((), ())), precision=lax.Precision.HIGHEST, preferred_element_type=F32
    )


def iota(shape, dim):
    return lax.broadcasted_iota(jnp.int32, shape, dim)


def wide(col, rows):
    return jnp.broadcast_to(col, (rows, L))


def place(row, col):
    return lax.axis_index("gy"), lax.axis_index("gx"), row[0], col[0]


def to_first(values, i):
    return pltpu.roll(values, L - i, 1) if i else values


def to_last(values, i):
    return pltpu.roll(values, L - 1 - i, 1) if i < L - 1 else values


def side_lane(x, ox):
    west = ox - 1 - L * x
    east = ox + SPAN - L * x
    is_west = (west >= 0) & (west < L)
    is_east = (east >= 0) & (east < L)
    return is_west, is_east, jnp.where(is_west, west, east)


def ring_row(g, x, oy):
    row = jnp.where(g == SOUTH, oy - 1, oy + SR) - PR * g
    ok = (row >= 0) & (row < PR) & (g >= SOUTH) & (g < GY - 1) & (x >= WEST) & (x < WEST + 12)
    return ok, row


def threes(x, shape, dim):
    cell = L * lax.rem(x, 3) + iota(shape, dim)
    first = 3 * iota(shape, 1 - dim)
    return ((first <= cell) & (cell < first + 3)).astype(F32)


def row_sums(rows, x):
    col = x * L + iota(rows.shape, 1)
    return exact(jnp.where((col > 0) & (col < GX * L - 1), rows, 0.0), threes(x, (L, L), 0))


def edge_kernel(o_row, o_col, a, nu, mask, traj, to_up, to_down, v_left, v_right, pay, row_s, col_s, buf, sems):
    g, x, oy, ox = place(o_row, o_col)
    row_ok, row = ring_row(g, x, oy)
    is_west, is_east, spot = side_lane(x, ox)
    side_ok = (is_west | is_east) & (g >= SOUTH) & (g < GY - 1)
    tile = pl.multiple_of(8 * (row // 8), 8)

    def row_copy():
        return pltpu.make_async_copy(traj.at[:, :, pl.ds(tile, 8), :], row_s, sems.at[2])

    def col_copy(s):
        return pltpu.make_async_copy(traj.at[s], col_s.at[s], sems.at[s])

    @pl.when(side_ok)
    def _():
        col_copy(1).start()
        col_copy(0).start()

    @pl.when(row_ok)
    def _():
        row_copy().start()

    m = mask[...].astype(F32)
    lane = iota((NR, L), 1)
    acc_l = jnp.zeros((NR, L), F32)
    acc_r = jnp.zeros((NR, L), F32)
    for k in range(K):
        v = nu[k] * m * a[k]
        to_up[pl.ds(k, 1), :] = v[0:1]
        to_down[pl.ds(k, 1), :] = v[NR - 1 : NR]
        acc_l = jnp.where(lane == k, pltpu.roll(v, k, 1) if k else v, acc_l)
        acc_r = jnp.where(lane == k, pltpu.roll(v, k + 1, 1), acc_r)
    v_left[...] = acc_l
    v_right[...] = acc_r
    pay[...] = jnp.zeros(pay.shape, F32)

    @pl.when(row_ok)
    def _():
        row_copy().wait()
        for i, s in enumerate((1, 0)):
            for k in range(K):
                pay[pl.ds(K * i + k, 1), :] = jax.nn.sigmoid(row_s[s, k, pl.ds(row - tile, 1), :])

    @pl.when(side_ok)
    def _():
        plane = iota((PR, L), 1)
        acc = jnp.zeros((PR, L), F32)
        for i, s in enumerate((1, 0)):
            col_copy(s).wait()
            for k in range(K):
                to = 64 * i + k
                acc = jnp.where(plane == to, pltpu.roll(col_s[s, k], lax.rem(to - spot + L, L), 1), acc)
        used = (plane < K) | ((plane >= 64) & (plane < 64 + K))
        buf[...] = jnp.zeros(buf.shape, F32)
        start = PR * g - oy + SR
        weights = jnp.where(used, jax.nn.sigmoid(acc), 0.0)
        for r in range(PR):
            buf[pl.ds(start + r, 1), :] = weights[r : r + 1]
        pay[104:168, :] = buf[SR : 2 * SR, :]

    for to in (to_up, to_down):
        to[K:56, :] = jnp.zeros((56 - K, L), F32)
    to_down[56:120, :] = pay[104:168, :]


def mix_kernel(o_col, pay, down, skip, after_left, after_right, after_up, after_base, *outs):
    g, x = lax.axis_index("gy"), lax.axis_index("gx")
    sig = o_col[0] - COL0
    own = pay[0:104, :] + jnp.where(g == 5, skip[0:104, :], 0.0)
    sides = pay[104:168, :] + down[56:120, :] + skip[104:168, :]
    lane = iota((K, L), 1)
    spare = jnp.zeros((64 - K, L), F32)
    for i, (t, out) in enumerate(zip(TURNS, outs)):
        begin = (0, 42, 85)[t % 3] - 1 + L * (t // 3) + sig
        turn = lax.rem(4 * L - begin, L)
        cell = begin + lane
        one = jnp.where((lane < 48) & (cell >= 0) & (cell < L), pltpu.roll(own[0:K], turn, 1), 0.0)
        cell = cell - 64
        two = jnp.where(
            (lane >= 64) & (lane < 112) & (cell >= 0) & (cell < L), pltpu.roll(own[K : 2 * K], lax.rem(turn + 64, L), 1), 0.0
        )
        part = jnp.concatenate([one + two, spare], 0)
        extra = g == 6
        for p, n in SEVENTH:
            extra = extra | ((g == 5) & (x == p) & (n == i))
        out[...] = jnp.where(extra, sides, part)


def base_kernel(o_row, o_col, q, pkappa, after, q_out, row_k, col_c, col_r, e_s, r_s):
    g, x, oy, ox = place(o_row, o_col)
    zero = jnp.zeros((PR, L), F32)
    src = q
    for step in (1, 0):
        c_prev, e_prev, y = zero, zero, zero
        for k in range(K):
            c = pkappa[step, k]
            r = 1.0 / (1.0 + c + c_prev * (1.0 - e_prev))
            e = c * r
            e_s[k] = e
            r_s[step, k] = r
            y = (src[k] + c_prev * y) * r
            q_out[k] = y
            c_prev, e_prev = c, e
        for k in range(K - 2, -1, -1):
            y = q_out[k] + e_s[k] * y
            q_out[k] = y
        src = q_out
    row_ok, row = ring_row(g, x, oy)
    is_west, is_east, spot = side_lane(x, ox)

    @pl.when(row_ok)
    def _():
        row_k[...] = pkappa[:, :, pl.ds(pl.multiple_of(8 * (row // 8), 8), 8), :]

    @pl.when(is_west | is_east)
    def _():
        lane = iota((PR, L), 1)
        for values, out in ((pkappa, col_c), (r_s, col_r)):
            acc = zero
            for i, s in enumerate((1, 0)):
                for k in range(K):
                    to = 64 * i + k
                    acc = jnp.where(lane == to, pltpu.roll(values[s, k], lax.rem(to - spot + L, L), 1), acc)
            out[...] = acc


def spread_kernel(side, v_left, v_right, down, up, after, out, one_s):
    x = lax.axis_index("gx")

    def packed(v):
        return v[0:12] + pltpu.roll(v[12:24], 64, 1)

    to_left, to_right = packed(v_left[...]), packed(v_right[...])
    one_s[0:K, :] = down[56 : 56 + K, :] + up[56 : 56 + K, :]
    one_s[K:62, :] = jnp.zeros((62 - K, L), F32)
    one_s[62:78, :] = side[...]
    one_s[78:80, :] = jnp.zeros((2, L), F32)
    every = one_s[...]
    for i in range(GX):
        out[i] = every

    @pl.when(x > 0)
    def _():
        out[jnp.maximum(x - 1, 0), K:62, :] = to_left

    @pl.when(x < GX - 1)
    def _():
        out[jnp.minimum(x + 1, GX - 1), K:62, :] = to_right


def turn_kernel(across, out):
    west, east = across[0, 62:78], across[GX - 1, 62:78]
    for i in range(GY):
        out[i, 0:16] = west
        out[i, 16:32] = east


def first_lane(t):
    return jnp.where(t == 0, 0, jnp.where(t == 1, 42, 85))


def nest_kernel(
    o_row, o_col, a, nu, mask, kappa, h_up, h_down, h_left, h_right, *rest,
):
    parts = rest[:7]
    a_out, to_up, to_down, v_left, v_right, side, e_s, y_s, w_s, up_s, down_s, g_s, we_s, w24_s = rest[8:]
    g, x, oy, ox = place(o_row, o_col)
    t = lax.rem(x, 3)
    def pick(i):
        got = jnp.where(t == 0, parts[i][...], parts[i + 1][...])
        return jnp.where(t == 2, parts[i + 2][...], got)

    window = (pick(0) + pick(3) + jnp.where(t == 2, parts[6][...], 0.0))[0:56]
    wl = iota((56, L), 1)
    low = wl < 64
    panel = jnp.concatenate([jnp.where(low, window, 0.0), jnp.where(low, pltpu.roll(window, 64, 1), 0.0)], 0)
    shift = first_lane(t) - 1
    si, sc = iota((L, L), 0) + shift, L * t + iota((L, L), 1)
    spread = ((3 * si <= sc) & (sc < 3 * si + 3)).astype(F32)
    c_all = x * L + iota((112, L), 1)
    inner = (c_all > 0) & (c_all < GX * L - 1) & ((g == 0) | (g == GY - 1))
    w_s[...] = jnp.where(inner, exact(panel, spread), 0.0)

    er, el = iota((8, L), 0), iota((8, L), 1)
    want = jnp.where(er == 0, jnp.where(t == 0, 0, 1), jnp.where(er == 1, jnp.where(t == 0, 43, 44), -1))
    ends = exact_t((el == want).astype(F32), panel[0:56])

    row24, lane24 = iota((NR, L), 0), iota((NR, L), 1)
    m_row = (((row24 == 0) & (g == 0)) | ((row24 == NR - 1) & (g == GY - 1))).astype(F32)
    m_lane = (((lane24 == 0) & (x == 0)) | ((lane24 == L - 1) & (x == GX - 1))).astype(F32)
    ends_l = jnp.concatenate([ends[0:1], jnp.zeros((1, L - 56), F32)], 1)
    ends_r = jnp.concatenate([ends[1:2], jnp.zeros((1, L - 56), F32)], 1)
    hl = h_left[...] * (1.0 - m_row * wide(ends_l, NR))
    hr = h_right[...] * (1.0 - m_row * wide(ends_r, NR))

    panel_we = jnp.zeros((SR, L), F32)
    for i, part in enumerate(parts):
        come = ((x == 0) & (side_round(0, g) == i)) | (
            (x == GX - 1) & ((side_round(1, g) == i) | (side_round(2, g) == i))
        )
        panel_we = panel_we + jnp.where(come, part[...], 0.0)
    we_s[...] = panel_we
    mine = we_s[pl.ds(pl.multiple_of(8 * g, 8), 8), :]
    for i in range(8):
        w24_s[3 * i : 3 * i + 3, :] = jnp.broadcast_to(mine[i : i + 1], (3, L))
    w_we = w24_s[...]
    flip = jnp.concatenate([panel_we, jnp.zeros((SR, L), F32)], 0).T[0:56]
    spot = jnp.where(x == 0, 0, L - 1)
    lane56 = iota((56, L), 1)
    edge = (lane56 == spot) & ((x == 0) | (x == GX - 1))
    w_up = jnp.where(edge & (g > 0), pltpu.roll(flip, lax.rem(spot - (8 * g - 1) + L, L), 1), 0.0)
    w_down = jnp.where(edge & (g < GY - 1), pltpu.roll(flip, lax.rem(spot - (8 * g + 8) + L, L), 1), 0.0)
    up_s[...] = h_up[0:K, :] * (1.0 - w_up[0:K])
    down_s[...] = h_down[0:K, :] * (1.0 - w_down[0:K])

    w_edge = jnp.where(x == 0, w_we, pltpu.roll(w_we, L - 1, 1))
    m = mask[...].astype(F32)
    one = jnp.ones((NR, L), F32)
    zero = jnp.zeros((NR, L), F32)
    c_prev, e_prev, y = zero, zero, zero
    top = g == 0
    side_ok = (x == 0) | (x == GX - 1)

    @pl.when(side_ok)
    def _():
        for k in range(K):
            y_s[k] = a[k] * (one - m_lane * to_first(w_edge, k))

    @pl.when(jnp.logical_not(side_ok))
    def _():
        y_s[...] = a[...]

    is31 = (x == GX - 1).astype(jnp.int32)
    for k in range(K):
        w_row = w_s[pl.ds(k, 1), :]
        raw = y_s[k]
        g_s[pl.ds(k, 1), :] = jnp.where(top, raw[0:1], raw[NR - 1 : NR])
        now = raw * (one - m_row * wide(w_row, NR))
        v = nu[k] * m * now
        above = jnp.where(row24 == 0, wide(up_s[pl.ds(k, 1), :], NR), pltpu.roll(v, 1, 0))
        below = jnp.where(row24 == NR - 1, wide(down_s[pl.ds(k, 1), :], NR), pltpu.roll(v, NR - 1, 0))
        left = jnp.where(lane24 == 0, to_first(hl, k), pltpu.roll(v, 1, 1))
        right = jnp.where(lane24 == L - 1, to_last(hr, k), pltpu.roll(v, L - 1, 1))
        b = m * (now + (above + below + left + right - 4.0 * v))
        c = kappa[1, k]
        r = 1.0 / (1.0 + c + c_prev * (1.0 - e_prev))
        e = c * r
        y = (b + c_prev * y) * r
        e_s[k] = e
        y_s[k] = y
        c_prev, e_prev = c, e
    sol = zero
    acc_l, acc_r = zero, zero
    for k in range(K - 1, -1, -1):
        sol = y_s[k] + e_s[k] * sol if k < K - 1 else y_s[k]
        y_s[k] = sol
    for k in range(K):
        sol = y_s[k]
        g_s[pl.ds(56 + k, 1), :] = jnp.where(top, sol[0:1], sol[NR - 1 : NR])
        a_out[k] = sol * (one - m_row * wide(w_s[pl.ds(56 + k, 1), :], NR))

    @pl.when(side_ok)
    def _():
        for k in range(K):
            a_out[k] = a_out[k] * (one - m_lane * to_first(w_edge, 64 + k))

    for k in range(K):
        v = nu[k] * m * a_out[k]
        to_up[pl.ds(k, 1), :] = v[0:1]
        to_down[pl.ds(k, 1), :] = v[NR - 1 : NR]
        acc_l = jnp.where(lane24 == k, pltpu.roll(v, k, 1) if k else v, acc_l)
        acc_r = jnp.where(lane24 == k, pltpu.roll(v, k + 1, 1), acc_r)
    v_left[...] = acc_l
    v_right[...] = acc_r
    for i in (*range(K, 56), *range(56 + K, 112)):
        g_s[pl.ds(i, 1), :] = jnp.zeros((1, L), F32)
    sums = row_sums(g_s[...], x)
    sums = pltpu.roll(sums, lax.rem(L - first_lane(t), L), 1)
    sums = sums[0:56] + pltpu.roll(sums[56:112], 64, 1)
    sums = jnp.where((g == 0) | (g == GY - 1), sums, 0.0)
    for to in (to_up, to_down):
        to[K:56, :] = jnp.zeros((56 - K, L), F32)
        to[56:112, :] = sums

    side[...] = jnp.zeros(side.shape, F32)

    @pl.when((x == 0) | (x == GX - 1))
    def _():
        acc = zero
        for k in range(K):
            acc = jnp.where(lane24 == k, pltpu.roll(a[k], lax.rem(k + is31, L), 1), acc)
            acc = jnp.where(lane24 == 64 + k, pltpu.roll(y_s[k], lax.rem(64 + k + is31, L), 1), acc)
        w24_s[...] = w_we * acc
        side[0:8, :] = w24_s[pl.ds(0, 8, 3), :] + w24_s[pl.ds(1, 8, 3), :] + w24_s[pl.ds(2, 8, 3), :]
        side[8:16, :] = mine


def inner_kernel(
    o_row, o_col, a, nu, mask, kappa, across, down, up, third, pay, row_k, q,
    a_out, q_out,
    e_s, g_s, t_s, up_s, tile_s, fact_s, sem,
):
    g, x, oy, ox = place(o_row, o_col)
    row_ok, row = ring_row(g, x, oy)
    tile = pl.multiple_of(8 * (row // 8), 8)
    at = pl.ds(tile, 8)

    def tile_copy():
        return pltpu.make_async_copy(q.at[:, at, :], tile_s, sem)

    @pl.when(row_ok)
    def _():
        tile_copy().start()

    m = mask[...].astype(F32)
    row24, lane24 = iota((NR, L), 0), iota((NR, L), 1)

    def unpacked(p):
        return jnp.concatenate([p, pltpu.roll(p, 64, 1)], 0)

    hl = jnp.where(x > 0, unpacked(across[jnp.maximum(x - 1, 0), K:62]), 0.0)
    hr = jnp.where(x < GX - 1, unpacked(across[jnp.minimum(x + 1, GX - 1), K:62]), 0.0)
    up_s[...] = third[...] + jnp.where((g == 4) | (g == 5), 0.0, down[0:K, :])
    zero = jnp.zeros((NR, L), F32)
    c_prev, e_prev, y = zero, zero, zero
    for k in range(K):
        now = a[k]
        v = nu[k] * m * now
        above = jnp.where(row24 == 0, wide(up_s[pl.ds(k, 1), :], NR), pltpu.roll(v, 1, 0))
        below = jnp.where(row24 == NR - 1, wide(up[pl.ds(k, 1), :], NR), pltpu.roll(v, NR - 1, 0))
        left = jnp.where(lane24 == 0, to_first(hl, k), pltpu.roll(v, 1, 1))
        right = jnp.where(lane24 == L - 1, to_last(hr, k), pltpu.roll(v, L - 1, 1))
        b = m * (now + (above + below + left + right - 4.0 * v))
        c = kappa[0, k]
        r = 1.0 / (1.0 + c + c_prev * (1.0 - e_prev))
        e = c * r
        y = (b + c_prev * y) * r
        e_s[k] = e
        a_out[k] = y
        c_prev, e_prev = c, e
    for k in range(K - 2, -1, -1):
        y = a_out[k] + e_s[k] * y
        a_out[k] = y

    @pl.when(row_ok)
    def _():
        sig = ox - COL0
        turn = lax.rem(sig, L)
        low = iota((56, L), 1) < 64

        def come(base):
            first = jnp.zeros((56, L), F32)
            second = jnp.zeros((56, L), F32)
            for t in range(3):
                j = 3 * base + t
                got = jnp.where((j >= 0) & (j < GX), across[jnp.clip(j, 0, GX - 1), 0:56], 0.0)
                one = jnp.where(low, got, 0.0)
                two = jnp.where(low, pltpu.roll(got, 64, 1), 0.0)
                start = (0, 42, 85)[t]
                first = first + (pltpu.roll(one, start, 1) if t else one)
                second = second + (pltpu.roll(two, start, 1) if t else two)
            return first, second

        def on_parent(own, prev):
            return jnp.where(iota(own.shape, 1) >= sig, pltpu.roll(own, turn, 1), pltpu.roll(prev, turn, 1))

        own, prev = come(x - WEST), come(x - WEST - 1)
        g_s[0:56, :] = on_parent(own[0], prev[0]) * pay[0:56, :]
        g_s[K : 2 * K, :] = on_parent(own[1], prev[1])[0:K] * pay[K : 2 * K, :]
        here = iota((8, L), 0) == row - tile
        zero = jnp.zeros((8, L), F32)
        for step in (1, 0):
            c_prev, e_prev, y = zero, zero, zero
            for k in range(K):
                c = row_k[step, k]
                r = 1.0 / (1.0 + c + c_prev * (1.0 - e_prev))
                e = c * r
                fact_s[k] = e
                term = jnp.where(here, wide(g_s[pl.ds(k if step else K + k, 1), :], 8), 0.0)
                y = ((term if step else term + t_s[k]) + c_prev * y) * r
                t_s[k] = y
                c_prev, e_prev = c, e
            for k in range(K - 2, -1, -1):
                y = t_s[k] + fact_s[k] * y
                t_s[k] = y
        tile_copy().wait()
        t_s[...] = t_s[...] + tile_s[...]
        back = pltpu.make_async_copy(t_s, q_out.at[:, at, :], sem)
        back.start()
        back.wait()


def outer_kernel(o_row, o_col, sides, col_c, col_r, q, q_out, s_w, s_g, panel_s, local_s, d_s, q_s, sems):
    g, x, oy, ox = place(o_row, o_col)
    is_west, is_east, spot = side_lane(x, ox)
    side_ok = (is_west | is_east) & (g >= SOUTH) & (g < GY - 1)

    def whole_copy():
        return pltpu.make_async_copy(q, q_s, sems.at[0])

    @pl.when(side_ok)
    def _():
        whole_copy().start()

    def panels(first):
        return jnp.concatenate([sides[i, 16 * e + first : 16 * e + first + 8, :] for e in (0, 1) for i in range(GY)], 0)

    grads = panels(0)
    flip_g = grads.T
    flip_w = panels(8).T
    for i, s in enumerate((1, 0)):
        for e in (0, 1):
            s_g[s, :, e, :] = flip_g[64 * i : 64 * i + K, SR * e : SR * e + SR]
            s_w[s, :, e, :] = flip_w[64 * i : 64 * i + K, SR * e : SR * e + SR]

    @pl.when(side_ok)
    def _():
        panel_s[...] = jnp.zeros(panel_s.shape, F32)
        panel_s[SR : 2 * SR, :] = jnp.where(is_west, grads[0:SR], grads[SR : 2 * SR])
        start = PR * g - oy + SR
        for r in range(PR):
            local_s[pl.ds(r, 1), :] = panel_s[pl.ds(start + r, 1), :]
        here = iota((PR, L), 1) == spot
        lane = iota((PR, L), 1)
        own = local_s[...]
        cs, rs = col_c[...], col_r[...]
        above = jnp.where((lane == 0) | (lane == 64), 0.0, pltpu.roll(cs, 1, 1)) * rs
        below = cs * rs
        own = own * rs
        own, above, below, rs = (pltpu.roll(v, spot, 1) for v in (own, above, below, rs))

        def column(values, i):
            return to_first(values, i)

        zero = jnp.zeros((PR, L), F32)
        for step, first in ((1, 0), (0, 64)):
            y = zero
            for k in range(K):
                term = column(own, first + k)
                if step == 0:
                    term = term + d_s[k] * column(rs, first + k)
                y = term + column(above, first + k) * y
                d_s[k] = y
            if step == 1:
                for k in range(K - 2, -1, -1):
                    y = d_s[k] + column(below, first + k) * y
                    d_s[k] = y
        whole_copy().wait()
        d_s[K - 1] = jnp.where(here, y, 0.0) + q_s[K - 1]
        copies = []
        for k in range(K - 2, -1, -1):
            y = d_s[k] + column(below, 64 + k) * y
            d_s[k] = jnp.where(here, y, 0.0) + q_s[k]
            if k % 10 == 0:
                part = pl.ds(k, 10)
                copies.append(pltpu.make_async_copy(d_s.at[part], q_out.at[part], sems.at[1 + k // 10]))
                copies[-1].start()
        for copy in copies:
            copy.wait()


def shape(*dims):
    return jax.ShapeDtypeStruct(dims, F32)


def at(g, x):
    return g * GX + x


def moved(value, pairs):
    return lax.ppermute(value, ("gy", "gx"), pairs)


def shifted(value, axis, count, step):
    pairs = [(i, i + step) for i in range(count) if 0 <= i + step < count]
    return lax.ppermute(value, axis, pairs)


def panel_routes():
    routes = []
    for t in TURNS:
        pairs = []
        for p in range(WEST, WEST + 12):
            j = 3 * (p - WEST) + t
            if 0 <= j < GX:
                pairs += [(at(4, p), at(0, j)), (at(5, p), at(7, j))]
        routes.append(pairs)
    for p, e, first in ((WEST, 0, 1), (WEST + 10, GX - 1, 3), (WEST + 11, GX - 1, 5)):
        for k in range(GY - 1):
            routes[(first + k) % 7].append((at(6, p), at(k, e)))
    for p, n in SEVENTH:
        routes[n].append((at(5, p), at(7, 0 if p == WEST else GX - 1)))
    return routes


def on_device(nest_adjoint, nest_kappa, nest_nu, land_mask, parent_adjoint, parent_kappa, parent_traj, offset_row, offset_col):
    here = (offset_row, offset_col)
    to_up, to_down, v_left, v_right, pay = pl.pallas_call(
        edge_kernel,
        out_shape=(shape(56, L), shape(120, L), shape(NR, L), shape(NR, L), shape(168, L)),
        in_specs=[SM] * 2 + [VM] * 3 + [HB],
        out_specs=(VM,) * 5,
        scratch_shapes=[
            pltpu.VMEM((2, K, 8, L), F32), pltpu.VMEM((2, K, PR, L), F32), pltpu.VMEM((256, L), F32),
            pltpu.SemaphoreType.DMA((3,)),
        ],
        compiler_params=grant(60),
        name="edge",
    )(*here, nest_adjoint, nest_nu, land_mask, parent_traj)
    down = shifted(to_down, "gy", GY, 1)
    up = shifted(to_up, "gy", GY, -1)
    ring = range(WEST, WEST + 12)
    skip = moved(
        pay, [(at(6, p), at(5, p)) for p in ring] + [(at(4, p), at(6, p)) for p in (WEST, WEST + 10, WEST + 11)]
    )
    h_left = shifted(v_right, "gx", GX, 1)
    h_right = shifted(v_left, "gx", GX, -1)
    nest, parent = shape(K, NR, L), shape(K, PR, L)
    base, row_k, col_c, col_r = pl.pallas_call(
        base_kernel,
        out_shape=(parent, shape(2, K, 8, L), shape(PR, L), shape(PR, L)),
        in_specs=[SM] * 2 + [VM] * 2 + [ANY],
        out_specs=(VM,) * 4,
        scratch_shapes=[pltpu.VMEM((K, PR, L), F32), pltpu.VMEM((2, K, PR, L), F32)],
        compiler_params=grant(16),
        cost_estimate=pl.CostEstimate(flops=10000000, bytes_accessed=12000000, transcendentals=0),
        name="base",
    )(*here, parent_adjoint, parent_kappa, v_left)
    mixed = pl.pallas_call(
        mix_kernel,
        out_shape=(shape(SR, L),) * 7,
        in_specs=[SM] + [VM] * 3 + [ANY] * 4,
        out_specs=(VM,) * 7,
        compiler_params=grant(4),
        name="mix",
    )(offset_col, pay, down, skip, h_left, h_right, up, col_c)
    parts = [moved(message, pairs) for message, pairs in zip(mixed, panel_routes())]
    state, to_up, to_down, v_left, v_right, side = pl.pallas_call(
        nest_kernel,
        out_shape=(nest, shape(112, L), shape(112, L), shape(NR, L), shape(NR, L), shape(16, L)),
        in_specs=[SM] * 2 + [VM] * 15 + [ANY],
        out_specs=(VM,) * 6,
        scratch_shapes=[
            pltpu.VMEM((K, NR, L), F32), pltpu.VMEM((K, NR, L), F32), pltpu.VMEM((112, L), F32), pltpu.VMEM((K, L), F32),
            pltpu.VMEM((K, L), F32), pltpu.VMEM((112, L), F32), pltpu.VMEM((SR, L), F32),
            pltpu.VMEM((NR, L), F32),
        ],
        compiler_params=grant(12),
        name="nest",
    )(*here, nest_adjoint, nest_nu, land_mask, nest_kappa, down, up, h_left, h_right, *parts, col_c)

    rows = ((0, 4), (7, 5), (1, 2), (2, 3), (5, 6), (6, 7))
    down = moved(to_down, [(at(i, j), at(k, j)) for i, k in rows for j in range(GX)])
    up = shifted(to_up, "gy", GY, -1)
    third = moved(to_down[0:K], [(at(i, j), at(i + 1, j)) for i in (0, 3, 4) for j in range(GX)])
    across = pl.pallas_call(
        spread_kernel,
        out_shape=shape(GX, 80, L),
        in_specs=[VM] * 5 + [ANY],
        out_specs=VM,
        scratch_shapes=[pltpu.VMEM((80, L), F32)],
        compiler_params=grant(4),
        name="spread",
    )(side, v_left, v_right, down, up, third)
    across = lax.all_to_all(across, "gx", 0, 0)
    sides = pl.pallas_call(
        turn_kernel, out_shape=shape(GY, 32, L), in_specs=[VM], out_specs=VM, compiler_params=grant(4), name="turn"
    )(across)
    sides = lax.all_to_all(sides, "gy", 0, 0)

    state, base = pl.pallas_call(
        inner_kernel,
        out_shape=(nest, parent),
        in_specs=[SM] * 2 + [VM] * 10 + [HB],
        out_specs=(VM, HB),
        scratch_shapes=[
            pltpu.VMEM((K, NR, L), F32), pltpu.VMEM((104, L), F32), pltpu.VMEM((K, 8, L), F32), pltpu.VMEM((K, L), F32),
            pltpu.VMEM((K, 8, L), F32), pltpu.VMEM((K, 8, L), F32), pltpu.SemaphoreType.DMA,
        ],
        input_output_aliases={12: 1},
        compiler_params=grant(14),
        name="inner",
    )(*here, state, nest_nu, land_mask, nest_kappa, across, down, up, third, pay, row_k, base)
    base, side_weights, side_gradients = pl.pallas_call(
        outer_kernel,
        out_shape=(parent, shape(2, K, 2, SR), shape(2, K, 2, SR)),
        in_specs=[SM] * 2 + [VM] * 3 + [HB],
        out_specs=(HB, VM, VM),
        scratch_shapes=[
            pltpu.VMEM((256, L), F32), pltpu.VMEM((PR, L), F32), pltpu.VMEM((K, PR, L), F32), pltpu.VMEM((K, PR, L), F32),
            pltpu.SemaphoreType.DMA((6,)),
        ],
        input_output_aliases={5: 0},
        compiler_params=grant(12),
        name="outer",
    )(*here, sides, col_c, col_r, base)
    return state, base, side_weights, side_gradients


def solution(mesh):
    in_specs = (
        P(None, "gy", "gx"),
        P(None, None, "gy", "gx"),
        P(None, "gy", "gx"),
        P("gy", "gx"),
        P(None, "gy", "gx"),
        P(None, None, "gy", "gx"),
        P(None, None, "gy", "gx"),
        P(),
        P(),
    )
    out_specs = (P(None, "gy", "gx"), P(None, "gy", "gx"), P(), P())
    return jax.shard_map(on_device, mesh=mesh, in_specs=in_specs, out_specs=out_specs, check_vma=False)
```

```python
import jax
import jax.numpy as jnp
from jax import lax
from jax.experimental import pallas as pl
from jax.experimental.pallas import tpu as pltpu
from jax.sharding import PartitionSpec as P

R = 3
K = 50
NR = 24
PR = 48
L = 128
GY = 8
GX = 32
SR = 64
ROW0 = 192
COL0 = 2048
SOUTH = 4
WEST = 16
SPAN = 1366
F32 = jnp.float32
VM = pl.BlockSpec(memory_space=pltpu.VMEM)
SM = pl.BlockSpec(memory_space=pltpu.SMEM)
HB = pl.BlockSpec(memory_space=pltpu.HBM)
ANY = pl.BlockSpec(memory_space=pl.ANY)


def grant(mib):
    return pltpu.CompilerParams(vmem_limit_bytes=mib * 1024 * 1024)


TURNS = (0, 1, 2, -3, -2, -1, -4)
SEVENTH = ((WEST, 4), (WEST + 10, 2), (WEST + 11, 0))


def side_round(i, g):
    return jnp.where(g == GY - 1, SEVENTH[i][1], lax.rem((1, 3, 5)[i] + g, 7))


def exact(left, right):
    return lax.dot_general(
        left, right, (((1,), (0,)), ((), ())), precision=lax.Precision.HIGHEST, preferred_element_type=F32
    )


def exact_t(left, right):
    return lax.dot_general(
        left, right, (((1,), (1,)), ((), ())), precision=lax.Precision.HIGHEST, preferred_element_type=F32
    )


def iota(shape, dim):
    return lax.broadcasted_iota(jnp.int32, shape, dim)


def wide(col, rows):
    return jnp.broadcast_to(col, (rows, L))


def place(row, col):
    return lax.axis_index("gy"), lax.axis_index("gx"), row[0], col[0]


def to_first(values, i):
    return pltpu.roll(values, L - i, 1) if i else values


def to_last(values, i):
    return pltpu.roll(values, L - 1 - i, 1) if i < L - 1 else values


def side_lane(x, ox):
    west = ox - 1 - L * x
    east = ox + SPAN - L * x
    is_west = (west >= 0) & (west < L)
    is_east = (east >= 0) & (east < L)
    return is_west, is_east, jnp.where(is_west, west, east)


def ring_row(g, x, oy):
    row = jnp.where(g == SOUTH, oy - 1, oy + SR) - PR * g
    ok = (row >= 0) & (row < PR) & (g >= SOUTH) & (g < GY - 1) & (x >= WEST) & (x < WEST + 12)
    return ok, row


def threes(x, shape, dim):
    cell = L * lax.rem(x, 3) + iota(shape, dim)
    first = 3 * iota(shape, 1 - dim)
    return ((first <= cell) & (cell < first + 3)).astype(F32)


def row_sums(rows, x):
    col = x * L + iota(rows.shape, 1)
    return exact(jnp.where((col > 0) & (col < GX * L - 1), rows, 0.0), threes(x, (L, L), 0))


def edge_kernel(o_row, o_col, a, nu, mask, traj, to_up, to_down, v_left, v_right, pay, row_s, col_s, buf, sems):
    g, x, oy, ox = place(o_row, o_col)
    row_ok, row = ring_row(g, x, oy)
    is_west, is_east, spot = side_lane(x, ox)
    side_ok = (is_west | is_east) & (g >= SOUTH) & (g < GY - 1)
    tile = pl.multiple_of(8 * (row // 8), 8)

    def row_copy():
        return pltpu.make_async_copy(traj.at[:, :, pl.ds(tile, 8), :], row_s, sems.at[2])

    def col_copy(s):
        return pltpu.make_async_copy(traj.at[s], col_s.at[s], sems.at[s])

    @pl.when(side_ok)
    def _():
        col_copy(1).start()
        col_copy(0).start()

    @pl.when(row_ok)
    def _():
        row_copy().start()

    m = mask[...].astype(F32)
    lane = iota((NR, L), 1)
    acc_l = jnp.zeros((NR, L), F32)
    acc_r = jnp.zeros((NR, L), F32)
    for k in range(K):
        v = nu[k] * m * a[k]
        to_up[pl.ds(k, 1), :] = v[0:1]
        to_down[pl.ds(k, 1), :] = v[NR - 1 : NR]
        acc_l = jnp.where(lane == k, pltpu.roll(v, k, 1) if k else v, acc_l)
        acc_r = jnp.where(lane == k, pltpu.roll(v, k + 1, 1), acc_r)
    v_left[...] = acc_l
    v_right[...] = acc_r
    pay[...] = jnp.zeros(pay.shape, F32)

    @pl.when(row_ok)
    def _():
        row_copy().wait()
        for i, s in enumerate((1, 0)):
            for k in range(K):
                pay[pl.ds(K * i + k, 1), :] = jax.nn.sigmoid(row_s[s, k, pl.ds(row - tile, 1), :])

    @pl.when(side_ok)
    def _():
        plane = iota((PR, L), 1)
        acc = jnp.zeros((PR, L), F32)
        for i, s in enumerate((1, 0)):
            col_copy(s).wait()
            for k in range(K):
                to = 64 * i + k
                acc = jnp.where(plane == to, pltpu.roll(col_s[s, k], lax.rem(to - spot + L, L), 1), acc)
        used = (plane < K) | ((plane >= 64) & (plane < 64 + K))
        buf[...] = jnp.zeros(buf.shape, F32)
        start = PR * g - oy + SR
        weights = jnp.where(used, jax.nn.sigmoid(acc), 0.0)
        for r in range(PR):
            buf[pl.ds(start + r, 1), :] = weights[r : r + 1]
        pay[104:168, :] = buf[SR : 2 * SR, :]

    for to in (to_up, to_down):
        to[K:56, :] = jnp.zeros((56 - K, L), F32)
    to_down[56:120, :] = pay[104:168, :]


def mix_kernel(o_col, pay, down, skip, after_left, after_right, *outs):
    g, x = lax.axis_index("gy"), lax.axis_index("gx")
    sig = o_col[0] - COL0
    own = pay[0:104, :] + jnp.where(g == 5, skip[0:104, :], 0.0)
    sides = pay[104:168, :] + down[56:120, :] + skip[104:168, :]
    lane = iota((K, L), 1)
    spare = jnp.zeros((64 - K, L), F32)
    for i, (t, out) in enumerate(zip(TURNS, outs)):
        begin = (0, 42, 85)[t % 3] - 1 + L * (t // 3) + sig
        turn = lax.rem(4 * L - begin, L)
        cell = begin + lane
        one = jnp.where((lane < 48) & (cell >= 0) & (cell < L), pltpu.roll(own[0:K], turn, 1), 0.0)
        cell = cell - 64
        two = jnp.where(
            (lane >= 64) & (lane < 112) & (cell >= 0) & (cell < L), pltpu.roll(own[K : 2 * K], lax.rem(turn + 64, L), 1), 0.0
        )
        part = jnp.concatenate([one + two, spare], 0)
        extra = g == 6
        for p, n in SEVENTH:
            extra = extra | ((g == 5) & (x == p) & (n == i))
        out[...] = jnp.where(extra, sides, part)


def base_kernel(o_row, o_col, q, pkappa, after, q_out, row_k, col_c, col_r, e_s, r_s):
    g, x, oy, ox = place(o_row, o_col)
    zero = jnp.zeros((PR, L), F32)
    src = q
    for step in (1, 0):
        c_prev, e_prev, y = zero, zero, zero
        for k in range(K):
            c = pkappa[step, k]
            r = 1.0 / (1.0 + c + c_prev * (1.0 - e_prev))
            e = c * r
            e_s[k] = e
            r_s[step, k] = r
            y = (src[k] + c_prev * y) * r
            q_out[k] = y
            c_prev, e_prev = c, e
        for k in range(K - 2, -1, -1):
            y = q_out[k] + e_s[k] * y
            q_out[k] = y
        src = q_out
    row_ok, row = ring_row(g, x, oy)
    is_west, is_east, spot = side_lane(x, ox)

    @pl.when(row_ok)
    def _():
        row_k[...] = pkappa[:, :, pl.ds(pl.multiple_of(8 * (row // 8), 8), 8), :]

    @pl.when(is_west | is_east)
    def _():
        lane = iota((PR, L), 1)
        for values, out in ((pkappa, col_c), (r_s, col_r)):
            acc = zero
            for i, s in enumerate((1, 0)):
                for k in range(K):
                    to = 64 * i + k
                    acc = jnp.where(lane == to, pltpu.roll(values[s, k], lax.rem(to - spot + L, L), 1), acc)
            out[...] = acc


def spread_kernel(side, v_left, v_right, down, up, after, out, one_s):
    x = lax.axis_index("gx")

    def packed(v):
        return v[0:12] + pltpu.roll(v[12:24], 64, 1)

    to_left, to_right = packed(v_left[...]), packed(v_right[...])
    one_s[0:K, :] = down[56 : 56 + K, :] + up[56 : 56 + K, :]
    one_s[K:62, :] = jnp.zeros((62 - K, L), F32)
    one_s[62:78, :] = side[...]
    one_s[78:80, :] = jnp.zeros((2, L), F32)
    every = one_s[...]
    for i in range(GX):
        out[i] = every

    @pl.when(x > 0)
    def _():
        out[jnp.maximum(x - 1, 0), K:62, :] = to_left

    @pl.when(x < GX - 1)
    def _():
        out[jnp.minimum(x + 1, GX - 1), K:62, :] = to_right


def turn_kernel(across, out):
    west, east = across[0, 62:78], across[GX - 1, 62:78]
    for i in range(GY):
        out[i, 0:16] = west
        out[i, 16:32] = east


def first_lane(t):
    return jnp.where(t == 0, 0, jnp.where(t == 1, 42, 85))


def nest_kernel(
    o_row, o_col, a, nu, mask, kappa, h_up, h_down, h_left, h_right, *rest,
):
    parts = rest[:7]
    a_out, to_up, to_down, v_left, v_right, side, e_s, y_s, w_s, up_s, down_s, g_s, we_s, w24_s = rest[8:]
    g, x, oy, ox = place(o_row, o_col)
    t = lax.rem(x, 3)
    def pick(i):
        got = jnp.where(t == 0, parts[i][...], parts[i + 1][...])
        return jnp.where(t == 2, parts[i + 2][...], got)

    window = (pick(0) + pick(3) + jnp.where(t == 2, parts[6][...], 0.0))[0:56]
    wl = iota((56, L), 1)
    low = wl < 64
    panel = jnp.concatenate([jnp.where(low, window, 0.0), jnp.where(low, pltpu.roll(window, 64, 1), 0.0)], 0)
    shift = first_lane(t) - 1
    si, sc = iota((L, L), 0) + shift, L * t + iota((L, L), 1)
    spread = ((3 * si <= sc) & (sc < 3 * si + 3)).astype(F32)
    c_all = x * L + iota((112, L), 1)
    inner = (c_all > 0) & (c_all < GX * L - 1) & ((g == 0) | (g == GY - 1))
    w_s[...] = jnp.where(inner, exact(panel, spread), 0.0)

    er, el = iota((8, L), 0), iota((8, L), 1)
    want = jnp.where(er == 0, jnp.where(t == 0, 0, 1), jnp.where(er == 1, jnp.where(t == 0, 43, 44), -1))
    ends = exact_t((el == want).astype(F32), panel[0:56])

    row24, lane24 = iota((NR, L), 0), iota((NR, L), 1)
    m_row = (((row24 == 0) & (g == 0)) | ((row24 == NR - 1) & (g == GY - 1))).astype(F32)
    m_lane = (((lane24 == 0) & (x == 0)) | ((lane24 == L - 1) & (x == GX - 1))).astype(F32)
    ends_l = jnp.concatenate([ends[0:1], jnp.zeros((1, L - 56), F32)], 1)
    ends_r = jnp.concatenate([ends[1:2], jnp.zeros((1, L - 56), F32)], 1)
    hl = h_left[...] * (1.0 - m_row * wide(ends_l, NR))
    hr = h_right[...] * (1.0 - m_row * wide(ends_r, NR))

    panel_we = jnp.zeros((SR, L), F32)
    for i, part in enumerate(parts):
        come = ((x == 0) & (side_round(0, g) == i)) | (
            (x == GX - 1) & ((side_round(1, g) == i) | (side_round(2, g) == i))
        )
        panel_we = panel_we + jnp.where(come, part[...], 0.0)
    we_s[...] = panel_we
    mine = we_s[pl.ds(pl.multiple_of(8 * g, 8), 8), :]
    for i in range(8):
        w24_s[3 * i : 3 * i + 3, :] = jnp.broadcast_to(mine[i : i + 1], (3, L))
    w_we = w24_s[...]
    flip = jnp.concatenate([panel_we, jnp.zeros((SR, L), F32)], 0).T[0:56]
    spot = jnp.where(x == 0, 0, L - 1)
    lane56 = iota((56, L), 1)
    edge = (lane56 == spot) & ((x == 0) | (x == GX - 1))
    w_up = jnp.where(edge & (g > 0), pltpu.roll(flip, lax.rem(spot - (8 * g - 1) + L, L), 1), 0.0)
    w_down = jnp.where(edge & (g < GY - 1), pltpu.roll(flip, lax.rem(spot - (8 * g + 8) + L, L), 1), 0.0)
    up_s[...] = h_up[0:K, :] * (1.0 - w_up[0:K])
    down_s[...] = h_down[0:K, :] * (1.0 - w_down[0:K])

    w_edge = jnp.where(x == 0, w_we, pltpu.roll(w_we, L - 1, 1))
    m = mask[...].astype(F32)
    one = jnp.ones((NR, L), F32)
    zero = jnp.zeros((NR, L), F32)
    c_prev, e_prev, y = zero, zero, zero
    top = g == 0
    side_ok = (x == 0) | (x == GX - 1)

    @pl.when(side_ok)
    def _():
        for k in range(K):
            y_s[k] = a[k] * (one - m_lane * to_first(w_edge, k))

    @pl.when(jnp.logical_not(side_ok))
    def _():
        y_s[...] = a[...]

    is31 = (x == GX - 1).astype(jnp.int32)
    for k in range(K):
        w_row = w_s[pl.ds(k, 1), :]
        raw = y_s[k]
        g_s[pl.ds(k, 1), :] = jnp.where(top, raw[0:1], raw[NR - 1 : NR])
        now = raw * (one - m_row * wide(w_row, NR))
        v = nu[k] * m * now
        above = jnp.where(row24 == 0, wide(up_s[pl.ds(k, 1), :], NR), pltpu.roll(v, 1, 0))
        below = jnp.where(row24 == NR - 1, wide(down_s[pl.ds(k, 1), :], NR), pltpu.roll(v, NR - 1, 0))
        left = jnp.where(lane24 == 0, to_first(hl, k), pltpu.roll(v, 1, 1))
        right = jnp.where(lane24 == L - 1, to_last(hr, k), pltpu.roll(v, L - 1, 1))
        b = m * (now + (above + below + left + right - 4.0 * v))
        c = kappa[1, k]
        r = 1.0 / (1.0 + c + c_prev * (1.0 - e_prev))
        e = c * r
        y = (b + c_prev * y) * r
        e_s[k] = e
        y_s[k] = y
        c_prev, e_prev = c, e
    sol = zero
    acc_l, acc_r = zero, zero
    for k in range(K - 1, -1, -1):
        sol = y_s[k] + e_s[k] * sol if k < K - 1 else y_s[k]
        y_s[k] = sol
    for k in range(K):
        sol = y_s[k]
        g_s[pl.ds(56 + k, 1), :] = jnp.where(top, sol[0:1], sol[NR - 1 : NR])
        a_out[k] = sol * (one - m_row * wide(w_s[pl.ds(56 + k, 1), :], NR))

    @pl.when(side_ok)
    def _():
        for k in range(K):
            a_out[k] = a_out[k] * (one - m_lane * to_first(w_edge, 64 + k))

    for k in range(K):
        v = nu[k] * m * a_out[k]
        to_up[pl.ds(k, 1), :] = v[0:1]
        to_down[pl.ds(k, 1), :] = v[NR - 1 : NR]
        acc_l = jnp.where(lane24 == k, pltpu.roll(v, k, 1) if k else v, acc_l)
        acc_r = jnp.where(lane24 == k, pltpu.roll(v, k + 1, 1), acc_r)
    v_left[...] = acc_l
    v_right[...] = acc_r
    for i in (*range(K, 56), *range(56 + K, 112)):
        g_s[pl.ds(i, 1), :] = jnp.zeros((1, L), F32)
    sums = row_sums(g_s[...], x)
    sums = pltpu.roll(sums, lax.rem(L - first_lane(t), L), 1)
    sums = sums[0:56] + pltpu.roll(sums[56:112], 64, 1)
    sums = jnp.where((g == 0) | (g == GY - 1), sums, 0.0)
    for to in (to_up, to_down):
        to[K:56, :] = jnp.zeros((56 - K, L), F32)
        to[56:112, :] = sums

    side[...] = jnp.zeros(side.shape, F32)

    @pl.when((x == 0) | (x == GX - 1))
    def _():
        acc = zero
        for k in range(K):
            acc = jnp.where(lane24 == k, pltpu.roll(a[k], lax.rem(k + is31, L), 1), acc)
            acc = jnp.where(lane24 == 64 + k, pltpu.roll(y_s[k], lax.rem(64 + k + is31, L), 1), acc)
        w24_s[...] = w_we * acc
        side[0:8, :] = w24_s[pl.ds(0, 8, 3), :] + w24_s[pl.ds(1, 8, 3), :] + w24_s[pl.ds(2, 8, 3), :]
        side[8:16, :] = mine


def inner_kernel(
    o_row, o_col, a, nu, mask, kappa, across, down, up, third, pay, row_k, q,
    a_out, q_out,
    e_s, g_s, t_s, up_s, tile_s, fact_s, sem,
):
    g, x, oy, ox = place(o_row, o_col)
    row_ok, row = ring_row(g, x, oy)
    tile = pl.multiple_of(8 * (row // 8), 8)
    at = pl.ds(tile, 8)

    def tile_copy():
        return pltpu.make_async_copy(q.at[:, at, :], tile_s, sem)

    @pl.when(row_ok)
    def _():
        tile_copy().start()

    m = mask[...].astype(F32)
    row24, lane24 = iota((NR, L), 0), iota((NR, L), 1)

    def unpacked(p):
        return jnp.concatenate([p, pltpu.roll(p, 64, 1)], 0)

    hl = jnp.where(x > 0, unpacked(across[jnp.maximum(x - 1, 0), K:62]), 0.0)
    hr = jnp.where(x < GX - 1, unpacked(across[jnp.minimum(x + 1, GX - 1), K:62]), 0.0)
    up_s[...] = third[...] + jnp.where((g == 4) | (g == 5), 0.0, down[0:K, :])
    zero = jnp.zeros((NR, L), F32)
    c_prev, e_prev, y = zero, zero, zero
    for k in range(K):
        now = a[k]
        v = nu[k] * m * now
        above = jnp.where(row24 == 0, wide(up_s[pl.ds(k, 1), :], NR), pltpu.roll(v, 1, 0))
        below = jnp.where(row24 == NR - 1, wide(up[pl.ds(k, 1), :], NR), pltpu.roll(v, NR - 1, 0))
        left = jnp.where(lane24 == 0, to_first(hl, k), pltpu.roll(v, 1, 1))
        right = jnp.where(lane24 == L - 1, to_last(hr, k), pltpu.roll(v, L - 1, 1))
        b = m * (now + (above + below + left + right - 4.0 * v))
        c = kappa[0, k]
        r = 1.0 / (1.0 + c + c_prev * (1.0 - e_prev))
        e = c * r
        y = (b + c_prev * y) * r
        e_s[k] = e
        a_out[k] = y
        c_prev, e_prev = c, e
    for k in range(K - 2, -1, -1):
        y = a_out[k] + e_s[k] * y
        a_out[k] = y

    @pl.when(row_ok)
    def _():
        sig = ox - COL0
        turn = lax.rem(sig, L)
        low = iota((56, L), 1) < 64

        def come(base):
            first = jnp.zeros((56, L), F32)
            second = jnp.zeros((56, L), F32)
            for t in range(3):
                j = 3 * base + t
                got = jnp.where((j >= 0) & (j < GX), across[jnp.clip(j, 0, GX - 1), 0:56], 0.0)
                one = jnp.where(low, got, 0.0)
                two = jnp.where(low, pltpu.roll(got, 64, 1), 0.0)
                start = (0, 42, 85)[t]
                first = first + (pltpu.roll(one, start, 1) if t else one)
                second = second + (pltpu.roll(two, start, 1) if t else two)
            return first, second

        def on_parent(own, prev):
            return jnp.where(iota(own.shape, 1) >= sig, pltpu.roll(own, turn, 1), pltpu.roll(prev, turn, 1))

        own, prev = come(x - WEST), come(x - WEST - 1)
        g_s[0:56, :] = on_parent(own[0], prev[0]) * pay[0:56, :]
        g_s[K : 2 * K, :] = on_parent(own[1], prev[1])[0:K] * pay[K : 2 * K, :]
        here = iota((8, L), 0) == row - tile
        zero = jnp.zeros((8, L), F32)
        for step in (1, 0):
            c_prev, e_prev, y = zero, zero, zero
            for k in range(K):
                c = row_k[step, k]
                r = 1.0 / (1.0 + c + c_prev * (1.0 - e_prev))
                e = c * r
                fact_s[k] = e
                term = jnp.where(here, wide(g_s[pl.ds(k if step else K + k, 1), :], 8), 0.0)
                y = ((term if step else term + t_s[k]) + c_prev * y) * r
                t_s[k] = y
                c_prev, e_prev = c, e
            for k in range(K - 2, -1, -1):
                y = t_s[k] + fact_s[k] * y
                t_s[k] = y
        tile_copy().wait()
        t_s[...] = t_s[...] + tile_s[...]
        back = pltpu.make_async_copy(t_s, q_out.at[:, at, :], sem)
        back.start()
        back.wait()


def outer_kernel(o_row, o_col, sides, col_c, col_r, q, q_out, s_w, s_g, panel_s, local_s, d_s, q_s, turned_s, y_s, sems):
    g, x, oy, ox = place(o_row, o_col)
    is_west, is_east, spot = side_lane(x, ox)
    side_ok = (is_west | is_east) & (g >= SOUTH) & (g < GY - 1)

    def whole_copy():
        return pltpu.make_async_copy(q, q_s, sems.at[0])

    @pl.when(side_ok)
    def _():
        whole_copy().start()

    def panels(first):
        return jnp.concatenate([sides[i, 16 * e + first : 16 * e + first + 8, :] for e in (0, 1) for i in range(GY)], 0)

    grads = panels(0)
    flip_g = grads.T
    flip_w = panels(8).T
    for i, s in enumerate((1, 0)):
        for e in (0, 1):
            s_g[s, :, e, :] = flip_g[64 * i : 64 * i + K, SR * e : SR * e + SR]
            s_w[s, :, e, :] = flip_w[64 * i : 64 * i + K, SR * e : SR * e + SR]

    @pl.when(side_ok)
    def _():
        panel_s[...] = jnp.zeros(panel_s.shape, F32)
        panel_s[SR : 2 * SR, :] = jnp.where(is_west, grads[0:SR], grads[SR : 2 * SR])
        start = PR * g - oy + SR
        for r in range(PR):
            local_s[pl.ds(r, 1), :] = panel_s[pl.ds(start + r, 1), :]
        here = iota((PR, L), 1) == spot
        lane = iota((PR, L), 1)
        own = local_s[...]
        cs, rs = col_c[...], col_r[...]
        above = jnp.where((lane == 0) | (lane == 64), 0.0, pltpu.roll(cs, 1, 1)) * rs
        below = cs * rs
        own = own * rs
        for i, values in enumerate((own, above, below, rs)):
            turned_s[i] = jnp.concatenate([values, jnp.zeros((L - PR, L), F32)], 0).T
        y_s[...] = jnp.zeros(y_s.shape, F32)

        def level(i, k):
            return turned_s[i, pl.ds(k, 1), :]

        for first in (0, 64):
            y = jnp.zeros((1, L), F32)
            for k in range(first, first + K):
                term = level(0, k)
                if first:
                    term = term + y_s[pl.ds(k - first, 1), :] * level(3, k)
                y = term + level(1, k) * y
                y_s[pl.ds(k, 1), :] = y
            for k in range(first + K - 2, first - 1, -1):
                y = y_s[pl.ds(k, 1), :] + level(2, k) * y
                y_s[pl.ds(k, 1), :] = y
        share = pltpu.roll(y_s[...].T[0:PR], spot, 1)
        whole_copy().wait()
        copies = []
        for k in range(K - 1, -1, -1):
            d_s[k] = jnp.where(here, to_first(share, 64 + k), 0.0) + q_s[k]
            if k % 10 == 0:
                part = pl.ds(k, 10)
                copies.append(pltpu.make_async_copy(d_s.at[part], q_out.at[part], sems.at[1 + k // 10]))
                copies[-1].start()
        for copy in copies:
            copy.wait()


def shape(*dims):
    return jax.ShapeDtypeStruct(dims, F32)


def at(g, x):
    return g * GX + x


def moved(value, pairs):
    return lax.ppermute(value, ("gy", "gx"), pairs)


def shifted(value, axis, count, step):
    pairs = [(i, i + step) for i in range(count) if 0 <= i + step < count]
    return lax.ppermute(value, axis, pairs)


def panel_routes():
    routes = []
    for t in TURNS:
        pairs = []
        for p in range(WEST, WEST + 12):
            j = 3 * (p - WEST) + t
            if 0 <= j < GX:
                pairs += [(at(4, p), at(0, j)), (at(5, p), at(7, j))]
        routes.append(pairs)
    for p, e, first in ((WEST, 0, 1), (WEST + 10, GX - 1, 3), (WEST + 11, GX - 1, 5)):
        for k in range(GY - 1):
            routes[(first + k) % 7].append((at(6, p), at(k, e)))
    for p, n in SEVENTH:
        routes[n].append((at(5, p), at(7, 0 if p == WEST else GX - 1)))
    return routes


def on_device(nest_adjoint, nest_kappa, nest_nu, land_mask, parent_adjoint, parent_kappa, parent_traj, offset_row, offset_col):
    here = (offset_row, offset_col)
    to_up, to_down, v_left, v_right, pay = pl.pallas_call(
        edge_kernel,
        out_shape=(shape(56, L), shape(120, L), shape(NR, L), shape(NR, L), shape(168, L)),
        in_specs=[SM] * 2 + [VM] * 3 + [HB],
        out_specs=(VM,) * 5,
        scratch_shapes=[
            pltpu.VMEM((2, K, 8, L), F32), pltpu.VMEM((2, K, PR, L), F32), pltpu.VMEM((256, L), F32),
            pltpu.SemaphoreType.DMA((3,)),
        ],
        compiler_params=grant(60),
        name="edge",
    )(*here, nest_adjoint, nest_nu, land_mask, parent_traj)
    down = shifted(to_down, "gy", GY, 1)
    up = shifted(to_up, "gy", GY, -1)
    ring = range(WEST, WEST + 12)
    skip = moved(
        pay, [(at(6, p), at(5, p)) for p in ring] + [(at(4, p), at(6, p)) for p in (WEST, WEST + 10, WEST + 11)]
    )
    h_left = shifted(v_right, "gx", GX, 1)
    h_right = shifted(v_left, "gx", GX, -1)
    mixed = pl.pallas_call(
        mix_kernel,
        out_shape=(shape(SR, L),) * 7,
        in_specs=[SM] + [VM] * 3 + [ANY] * 2,
        out_specs=(VM,) * 7,
        compiler_params=grant(4),
        name="mix",
    )(offset_col, pay, down, skip, h_left, h_right)
    parts = [moved(message, pairs) for message, pairs in zip(mixed, panel_routes())]
    nest, parent = shape(K, NR, L), shape(K, PR, L)
    base, row_k, col_c, col_r = pl.pallas_call(
        base_kernel,
        out_shape=(parent, shape(2, K, 8, L), shape(PR, L), shape(PR, L)),
        in_specs=[SM] * 2 + [VM] * 2 + [ANY],
        out_specs=(VM,) * 4,
        scratch_shapes=[pltpu.VMEM((K, PR, L), F32), pltpu.VMEM((2, K, PR, L), F32)],
        compiler_params=grant(16),
        cost_estimate=pl.CostEstimate(flops=10000000, bytes_accessed=12000000, transcendentals=0),
        name="base",
    )(*here, parent_adjoint, parent_kappa, mixed[6])

    state, to_up, to_down, v_left, v_right, side = pl.pallas_call(
        nest_kernel,
        out_shape=(nest, shape(112, L), shape(112, L), shape(NR, L), shape(NR, L), shape(16, L)),
        in_specs=[SM] * 2 + [VM] * 15 + [ANY],
        out_specs=(VM,) * 6,
        scratch_shapes=[
            pltpu.VMEM((K, NR, L), F32), pltpu.VMEM((K, NR, L), F32), pltpu.VMEM((112, L), F32), pltpu.VMEM((K, L), F32),
            pltpu.VMEM((K, L), F32), pltpu.VMEM((112, L), F32), pltpu.VMEM((SR, L), F32),
            pltpu.VMEM((NR, L), F32),
        ],
        compiler_params=grant(12),
        name="nest",
    )(*here, nest_adjoint, nest_nu, land_mask, nest_kappa, down, up, h_left, h_right, *parts, col_c)

    rows = ((0, 4), (7, 5), (1, 2), (2, 3), (5, 6), (6, 7))
    down = moved(to_down, [(at(i, j), at(k, j)) for i, k in rows for j in range(GX)])
    up = shifted(to_up, "gy", GY, -1)
    third = moved(to_down[0:K], [(at(i, j), at(i + 1, j)) for i in (0, 3, 4) for j in range(GX)])
    across = pl.pallas_call(
        spread_kernel,
        out_shape=shape(GX, 80, L),
        in_specs=[VM] * 5 + [ANY],
        out_specs=VM,
        scratch_shapes=[pltpu.VMEM((80, L), F32)],
        compiler_params=grant(4),
        name="spread",
    )(side, v_left, v_right, down, up, third)
    across = lax.all_to_all(across, "gx", 0, 0)
    sides = pl.pallas_call(
        turn_kernel, out_shape=shape(GY, 32, L), in_specs=[VM], out_specs=VM, compiler_params=grant(4), name="turn"
    )(across)
    sides = lax.all_to_all(sides, "gy", 0, 0)

    state, base = pl.pallas_call(
        inner_kernel,
        out_shape=(nest, parent),
        in_specs=[SM] * 2 + [VM] * 10 + [HB],
        out_specs=(VM, HB),
        scratch_shapes=[
            pltpu.VMEM((K, NR, L), F32), pltpu.VMEM((104, L), F32), pltpu.VMEM((K, 8, L), F32), pltpu.VMEM((K, L), F32),
            pltpu.VMEM((K, 8, L), F32), pltpu.VMEM((K, 8, L), F32), pltpu.SemaphoreType.DMA,
        ],
        input_output_aliases={12: 1},
        compiler_params=grant(14),
        name="inner",
    )(*here, state, nest_nu, land_mask, nest_kappa, across, down, up, third, pay, row_k, base)
    base, side_weights, side_gradients = pl.pallas_call(
        outer_kernel,
        out_shape=(parent, shape(2, K, 2, SR), shape(2, K, 2, SR)),
        in_specs=[SM] * 2 + [VM] * 3 + [HB],
        out_specs=(HB, VM, VM),
        scratch_shapes=[
            pltpu.VMEM((256, L), F32), pltpu.VMEM((PR, L), F32), pltpu.VMEM((K, PR, L), F32), pltpu.VMEM((K, PR, L), F32),
            pltpu.VMEM((4, L, L), F32), pltpu.VMEM((L, L), F32), pltpu.SemaphoreType.DMA((6,)),
        ],
        input_output_aliases={5: 0},
        compiler_params=grant(12),
        name="outer",
    )(*here, sides, col_c, col_r, base)
    return state, base, side_weights, side_gradients


def solution(mesh):
    in_specs = (
        P(None, "gy", "gx"),
        P(None, None, "gy", "gx"),
        P(None, "gy", "gx"),
        P("gy", "gx"),
        P(None, "gy", "gx"),
        P(None, None, "gy", "gx"),
        P(None, None, "gy", "gx"),
        P(),
        P(),
    )
    out_specs = (P(None, "gy", "gx"), P(None, "gy", "gx"), P(), P())
    return jax.shard_map(on_device, mesh=mesh, in_specs=in_specs, out_specs=out_specs, check_vma=False)
```
